256 devices in a mesh: blk: 128 (over x, z, y_hi, core), half: 2 (over y_lo).
Axes of the slice: x: 4, y: 4 (y_hi: 2, y_lo: 2; y = y_hi * 2 + y_lo), z: 8, core: 2. Of those that a mesh axis runs over, the one named last changes fastest.
Arguments:
- points: float32 [32, 393216], P(None, ('blk', 'half')), may hold values from -6 to 6
- vectors: float32 [17, 393216], P(None, ('blk', 'half')), may hold values from -6 to 6
- inv_length: float32 [32], replicated, may hold values from 0.12 to 0.35
- signal_var: float32 [1], replicated, may hold values from 0.02 to 0.1
- noise_var: float32 [1], replicated, may hold values from 0.05 to 0.5
- masks: int32 [3], replicated, may hold values from 1 to 127, as said below
Outputs:
- product: float32 [17, 393216], P(None, ('blk', 'half'))
The draws below stay inside these ranges and needn't reach their ends.
Inputs may be any that keep to these rules, and one draw needn't show every extreme that they name: `masks`: the entries are distinct; one of them is 1 and one is 127.
All inputs are finite; a program needn't handle non-finite values.
Results may differ from the reference program's by a relative error of at most 0.0003.
Values sent between devices are 32-bit elements; how exact they have to be, the bound alone decides.
A program may use at most 64 MiB of HBM per device.

```python
import math
import jax
import jax.numpy as jnp
from jax import lax

D = 32
R = 17
ROUNDS = 3
BLOCKS = 128
BLOCK_PTS = 3072
NPTS = 393216


def draw_masks(key, part):
    key = jax.random.fold_in(key, 7)
    first_key, second_key = jax.random.split(key)
    middle = jax.random.permutation(first_key, BLOCKS - 3)[:ROUNDS - 2] + 2
    values = jnp.concatenate([jnp.array([1, BLOCKS - 1], jnp.int32), middle.astype(jnp.int32)])
    order = jax.random.permutation(second_key, ROUNDS)
    return values[order]


def block_levels(own_key, shape, shards, low, largest):
    def one(axis_at, blocks):
        heights = jax.random.uniform(jax.random.fold_in(jax.random.fold_in(own_key, 6), axis_at), (blocks,), jnp.float32, low / len(shards), largest / len(shards))
        return jnp.repeat(jnp.exp(heights), shape[axis_at] // blocks).reshape((-1,) + (1,) * (len(shape) - axis_at - 1))

    level = one(*shards[0])
    for cut in shards[1:]:
        level = level * one(*cut)
    return level


def bell_draw(stream_key, extent, width, most, pieces=(), held_as=jnp.bfloat16):
    drawn = jax.random.normal(stream_key, extent, jnp.float32) * width
    if len(pieces) > 0:
        drawn = block_levels(stream_key, extent, pieces, -0.22, 0.18) * drawn
    return jnp.clip(drawn, min=-most, max=most).astype(held_as)


def setup_inputs(seed: int = 0) -> dict:
    seeds = jax.random.split(jax.random.key(seed), 7)
    points = bell_draw(seeds[0], (D, NPTS), 1.0, 6.0, ((1, 256),), jnp.float32)
    vectors = bell_draw(seeds[1], (R, NPTS), 1.0, 6.0, ((1, 256),), jnp.float32)
    inv_length = jnp.clip(jnp.exp(jax.random.uniform(seeds[2], (D,), jnp.float32, math.log(0.12), math.log(0.35))), 0.12, 0.35)
    signal_var = jnp.clip(jnp.exp(jax.random.uniform(seeds[3], (1,), jnp.float32, math.log(0.02), math.log(0.1))), 0.02, 0.1)
    noise_var = jnp.clip(jnp.exp(jax.random.uniform(seeds[4], (1,), jnp.float32, math.log(0.05), math.log(0.5))), 0.05, 0.5)
    masks = draw_masks(jax.random.fold_in(seeds[6], 71), 0)
    return {"points": points, "vectors": vectors, "inv_length": inv_length, "signal_var": signal_var, "noise_var": noise_var, "masks": masks}


SQRT_FIVE = math.sqrt(5.0)

def matern(squared):
    distance = SQRT_FIVE * jnp.sqrt(jnp.maximum(squared, 0.0))
    return (1.0 + distance + distance * distance / 3.0) * jnp.exp(-distance)

def block_terms(rows, columns, column_vectors):
    row_norm = lax.optimization_barrier(jnp.sum(rows * rows, axis=0))
    column_norm = lax.optimization_barrier(jnp.sum(columns * columns, axis=0))
    inner = jnp.dot(rows.T, columns, precision=lax.Precision.HIGHEST)
    kernel = matern(row_norm[:, None] + column_norm[None, :] - 2.0 * inner)
    return lax.dot_general(column_vectors, kernel, (((1,), (1,)), ((), ())), precision=lax.Precision.HIGHEST)

def reference(points, vectors, inv_length, signal_var, noise_var, masks):
    scaled = points * inv_length[:, None]
    feature_blocks = scaled.reshape(D, BLOCKS, BLOCK_PTS).transpose(1, 0, 2)
    vector_blocks = vectors.reshape(R, BLOCKS, BLOCK_PTS).transpose(1, 0, 2)

    def one_block(block_index):
        rows = feature_blocks[block_index]
        summed = block_terms(rows, rows, vector_blocks[block_index])
        for which_round in range(ROUNDS):
            partner = jnp.bitwise_xor(block_index, masks[which_round]).astype(jnp.int32)
            summed = summed + block_terms(rows, feature_blocks[partner], vector_blocks[partner])
        return summed
    sums = lax.map(one_block, jnp.arange(BLOCKS, dtype=jnp.int32))
    sums = sums.transpose(1, 0, 2).reshape(R, NPTS)
    return signal_var[0] * sums + noise_var[0] * vectors
```

```python
import functools
import math

import jax
import jax.numpy as jnp
from jax import lax
from jax.experimental import pallas as pl
from jax.experimental.pallas import tpu as pltpu
from jax.sharding import PartitionSpec as P

F32 = jnp.float32
BF16 = jnp.bfloat16
LOW = jnp.float8_e5m2
LOG2E = math.log2(math.e)
ALPHA = 1.5 * LOG2E
BETA = 0.75 * LOG2E * LOG2E
FACTOR = math.exp(1.5) / (3.0 * LOG2E * LOG2E)
STRETCH = math.sqrt(5.0) * LOG2E
TINY = 1e-30
DEPTH = 256
COLUMNS = 256


def pieces(x, count):
    out = []
    for _ in range(count):
        part = x.astype(BF16).astype(F32)
        out.append(part)
        x = x - part
    return out


def features(points, inv):
    x = points * inv
    norm = jnp.sum(x * x, axis=0, keepdims=True)
    return pieces(x, 3), pieces(norm, 3)


def row_side(points, inv):
    (h, m, l), norm = features(points, inv)
    one = jnp.ones_like(norm[0])
    tail = jnp.concatenate(norm + [one, one, one], axis=0)
    rest = jnp.zeros((DEPTH - 198, points.shape[1]), F32)
    return jnp.concatenate([-2.0 * p for p in (h, h, m, h, l, m)] + [tail, rest], axis=0).astype(BF16)


def column_side(points, inv):
    (h, m, l), norm = features(points, inv)
    one = jnp.ones_like(norm[0])
    tail = jnp.concatenate([one, one, one] + norm, axis=0)
    rest = jnp.zeros((DEPTH - 198, points.shape[1]), F32)
    return jnp.concatenate([h, m, h, l, h, m, tail, rest], axis=0).astype(BF16)


def vector_side(vectors):
    pad = jnp.zeros((7, vectors.shape[1]), F32)
    hi, lo = pieces(vectors, 2)
    wide = jnp.concatenate([hi, pad, lo, pad], axis=0).astype(BF16)
    first = vectors.astype(LOW).astype(F32)
    second = vectors - first
    fill = jnp.zeros((16, vectors.shape[1]), F32)
    low = jnp.concatenate([first, pad, second, pad, fill], axis=0).astype(LOW)
    return wide, low


def kernel_values(squared):
    q = jnp.maximum(squared, TINY)
    h = -ALPHA - q * lax.rsqrt(q)
    values = (h * h + BETA) * jnp.exp2(h)
    hi = values.astype(BF16)
    return hi, (values - hi.astype(F32)).astype(LOW)


def dot(a, b):
    return jnp.dot(a, b, preferred_element_type=F32)


def dot_t(a, b):
    return lax.dot_general(a, b, (((1,), (1,)), ((), ())), preferred_element_type=F32)


def folded(wide, low):
    return wide[0:24] + wide[24:48] + low[0:24] + low[24:48]


def one_way_body(source, mine, inv, out, rows, cols, vec, vec_low):
    n = mine.shape[1]
    rows[...] = row_side(source[0:32, :], inv[...]).T
    cols[...] = column_side(mine[0:32, :], inv[...])
    vec[...], vec_low[...] = vector_side(source[32:49, :])

    def step(i, carry):
        c = pl.ds(pl.multiple_of(i * COLUMNS, COLUMNS), COLUMNS)
        hi, lo = kernel_values(dot(rows[...], cols[:, c]))
        out[:, c] = folded(dot(vec[...], hi), dot(vec_low[...], lo))[0:17]
        return carry

    lax.fori_loop(0, n // COLUMNS, step, 0)


def two_way_body(flag, other, mine, spare, inv, own, par, rows, cols, vec, vec_low, vec_o, vec_o_low, acc, acc_low):
    n = mine.shape[1]
    base = jnp.where(flag[0] == 1, spare[...], mine[...])
    rows[...] = row_side(base[0:32, :], inv[...]).T
    cols[...] = column_side(other[0:32, :], inv[...])
    vec[...], vec_low[...] = vector_side(base[32:49, :])
    vec_o[...], vec_o_low[...] = vector_side(other[32:49, :])
    acc[...] = jnp.zeros_like(acc)
    acc_low[...] = jnp.zeros_like(acc_low)

    def step(i, carry):
        c = pl.ds(pl.multiple_of(i * COLUMNS, COLUMNS), COLUMNS)
        hi, lo = kernel_values(dot(rows[...], cols[:, c]))
        par[:, c] = folded(dot(vec[...], hi), dot(vec_low[...], lo))[0:17]
        acc[...] += dot_t(vec_o[:, c], hi)
        acc_low[...] += dot_t(vec_o_low[:, c], lo)
        return carry

    lax.fori_loop(0, n // COLUMNS, step, 0)
    own[...] = folded(acc[...], acc_low[...])[0:17]


def operands(n):
    return [
        pltpu.VMEM((n, DEPTH), BF16),
        pltpu.VMEM((DEPTH, n), BF16),
        pltpu.VMEM((48, n), BF16),
        pltpu.VMEM((64, n), LOW),
    ]


def estimate(n, passes):
    return pl.CostEstimate(flops=2 * n * n * 256 * passes, bytes_accessed=4 * 115 * n, transcendentals=2 * n * n)


def one_way(source, mine, inv):
    n = mine.shape[1]
    return pl.pallas_call(
        one_way_body,
        out_shape=jax.ShapeDtypeStruct((17, n), F32),
        scratch_shapes=operands(n),
        cost_estimate=estimate(n, 10),
        compiler_params=pltpu.CompilerParams(vmem_limit_bytes=48 << 20),
    )(source, mine, inv)


def two_way(flag, other, mine, spare, inv):
    n = mine.shape[1]
    shape = jax.ShapeDtypeStruct((17, n), F32)
    whole = pl.BlockSpec(memory_space=pltpu.VMEM)
    return pl.pallas_call(
        two_way_body,
        out_shape=(shape, shape),
        in_specs=[pl.BlockSpec(memory_space=pltpu.SMEM)] + [whole] * 4,
        scratch_shapes=operands(n)
        + [
            pltpu.VMEM((48, n), BF16),
            pltpu.VMEM((64, n), LOW),
            pltpu.VMEM((48, n), F32),
            pltpu.VMEM((64, n), F32),
        ],
        cost_estimate=estimate(n, 20),
        compiler_params=pltpu.CompilerParams(vmem_limit_bytes=48 << 20),
    )(flag, other, mine, spare, inv)


AXES = ("blk", "half")


def fetch_pairs(mask, blocks):
    top = mask.bit_length() - 1
    pairs = []
    for block in range(blocks):
        for half in range(2):
            side = half ^ (block >> top & 1)
            if mask % 2 == 0:
                side ^= block & 1
            pairs.append(((block ^ mask) * 2 + side, block * 2 + half))
    return pairs


def back(pairs):
    return [(b, a) for a, b in pairs]


def local(points, vectors, inv_length, signal_var, noise_var, masks):
    inv = (inv_length * STRETCH)[:, None]
    mine = jnp.concatenate([points, vectors], axis=0)
    blocks = lax.axis_size("blk")
    last = blocks - 1
    middle = masks[0] ^ masks[1] ^ masks[2] ^ 1 ^ last
    odd = middle & 1
    which = (middle >> 1) - 1
    routes = [fetch_pairs(m, blocks) for m in range(2, blocks, 2)]
    far_pairs, near_pairs = fetch_pairs(last, blocks), fetch_pairs(1, blocks)
    zero = jnp.zeros((1,), jnp.int32)

    far = lax.ppermute(mine, AXES, far_pairs)
    near = lax.ppermute(mine, AXES, near_pairs)
    sibling = lax.ppermute(mine, "half", [(0, 1), (1, 0)])
    mid = lax.switch(which, [lambda x, p=p: lax.ppermute(x, AXES, p) for p in routes], mine)
    total = one_way(mine, mine, inv)
    own_near, par_near = two_way(zero, near, mine, mine, inv)
    own_mid, par_mid = two_way(odd.reshape(1), mid, mine, near, inv)
    back_mid = lax.switch(which, [lambda x, p=p: lax.ppermute(x, AXES, back(p)) for p in routes], par_mid)
    back_near = lax.ppermute(par_near + jnp.where(odd == 1, own_mid, 0.0), AXES, back(near_pairs))
    own_far, par_far = two_way(zero, far, mine, mine, inv)
    back_far = lax.ppermute(par_far, AXES, back(far_pairs))
    total_sibling = one_way(sibling, mine, inv)
    sums = total + total_sibling + own_near + jnp.where(odd == 1, 0.0, own_mid) + own_far + back_near + back_mid + back_far
    return (signal_var[0] * FACTOR) * sums + noise_var[0] * vectors


def solution(mesh):
    return jax.shard_map(
        local,
        mesh=mesh,
        in_specs=(P(None, AXES), P(None, AXES), P(), P(), P(), P()),
        out_specs=P(None, AXES),
        check_vma=False,
    )
```

```python
import functools
import math

import jax
import jax.numpy as jnp
import numpy as np
from jax import lax
from jax.experimental import pallas as pl
from jax.experimental.pallas import tpu as pltpu
from jax.sharding import PartitionSpec as P

F32 = jnp.float32
BF16 = jnp.bfloat16
LOW = jnp.float8_e5m2
LOG2E = math.log2(math.e)
ALPHA = 1.5 * LOG2E
BETA = 0.75 * LOG2E * LOG2E
FACTOR = math.exp(1.5) / (3.0 * LOG2E * LOG2E)
STRETCH = math.sqrt(5.0) * LOG2E
TINY = 1e-30
DEPTH = 256
COLUMNS = 256


def pieces(x, count):
    out = []
    for _ in range(count):
        part = x.astype(BF16).astype(F32)
        out.append(part)
        x = x - part
    return out


def features(points, inv):
    x = points * inv
    norm = jnp.sum(x * x, axis=0, keepdims=True)
    return pieces(x, 3), pieces(norm, 3)


def row_side(points, inv):
    (h, m, l), norm = features(points, inv)
    one = jnp.ones_like(norm[0])
    tail = jnp.concatenate(norm + [one, one, one], axis=0)
    rest = jnp.zeros((DEPTH - 198, points.shape[1]), F32)
    return jnp.concatenate([-2.0 * p for p in (h, h, m, h, l, m)] + [tail, rest], axis=0).astype(BF16)


def column_side(points, inv):
    (h, m, l), norm = features(points, inv)
    one = jnp.ones_like(norm[0])
    tail = jnp.concatenate([one, one, one] + norm, axis=0)
    rest = jnp.zeros((DEPTH - 198, points.shape[1]), F32)
    return jnp.concatenate([h, m, h, l, h, m, tail, rest], axis=0).astype(BF16)


def vector_side(vectors):
    pad = jnp.zeros((7, vectors.shape[1]), F32)
    hi, lo = pieces(vectors, 2)
    wide = jnp.concatenate([hi, pad, lo, pad], axis=0).astype(BF16)
    first = vectors.astype(LOW).astype(F32)
    second = vectors - first
    fill = jnp.zeros((16, vectors.shape[1]), F32)
    low = jnp.concatenate([first, pad, second, pad, fill], axis=0).astype(LOW)
    return wide, low


def kernel_values(squared):
    q = jnp.maximum(squared, TINY)
    h = -ALPHA - q * lax.rsqrt(q)
    values = (h * h + BETA) * jnp.exp2(h)
    hi = values.astype(BF16)
    return hi, (values - hi.astype(F32)).astype(LOW)


def dot(a, b):
    return jnp.dot(a, b, preferred_element_type=F32)


def dot_t(a, b):
    return lax.dot_general(a, b, (((1,), (1,)), ((), ())), preferred_element_type=F32)


def folded(wide, low):
    return wide[0:24] + wide[24:48] + low[0:24] + low[24:48]


def one_way_body(source, mine, inv, out, rows, cols, vec, vec_low):
    n = mine.shape[1]
    rows[...] = row_side(source[0:32, :], inv[...]).T
    cols[...] = column_side(mine[0:32, :], inv[...])
    vec[...], vec_low[...] = vector_side(source[32:49, :])

    def step(i, carry):
        c = pl.ds(pl.multiple_of(i * COLUMNS, COLUMNS), COLUMNS)
        hi, lo = kernel_values(dot(rows[...], cols[:, c]))
        out[:, c] = folded(dot(vec[...], hi), dot(vec_low[...], lo))[0:17]
        return carry

    lax.fori_loop(0, n // COLUMNS, step, 0)


def two_way_body(*refs, count):
    other, sides, inv = refs[0], refs[1 : 1 + count], refs[1 + count]
    sums, par = refs[2 + count : 2 + 2 * count], refs[2 + 2 * count]
    rows, cols, vec, vec_low, vec_o, vec_o_low, acc, acc_low = refs[3 + 2 * count :]
    n = other.shape[1]
    cols[...] = column_side(other[0:32, :], inv[...])
    vec_o[...], vec_o_low[...] = vector_side(other[32:49, :])
    for k, (side, total) in enumerate(zip(sides, sums)):
        rows[...] = row_side(side[0:32, :], inv[...]).T
        vec[...], vec_low[...] = vector_side(side[32:49, :])
        acc[...] = jnp.zeros_like(acc)
        acc_low[...] = jnp.zeros_like(acc_low)

        def step(i, carry):
            c = pl.ds(pl.multiple_of(i * COLUMNS, COLUMNS), COLUMNS)
            hi, lo = kernel_values(dot(rows[...], cols[:, c]))
            part = folded(dot(vec[...], hi), dot(vec_low[...], lo))[0:17]
            par[:, c] = part if k == 0 else par[:, c] + part
            acc[...] += dot_t(vec_o[:, c], hi)
            acc_low[...] += dot_t(vec_o_low[:, c], lo)
            return carry

        lax.fori_loop(0, n // COLUMNS, step, 0)
        total[...] = folded(acc[...], acc_low[...])[0:17]


def operands(n):
    return [
        pltpu.VMEM((n, DEPTH), BF16),
        pltpu.VMEM((DEPTH, n), BF16),
        pltpu.VMEM((48, n), BF16),
        pltpu.VMEM((64, n), LOW),
    ]


def estimate(n, passes):
    return pl.CostEstimate(flops=2 * n * n * 256 * passes, bytes_accessed=4 * 115 * n, transcendentals=2 * n * n)


def one_way(source, mine, inv):
    n = mine.shape[1]
    return pl.pallas_call(
        one_way_body,
        out_shape=jax.ShapeDtypeStruct((17, n), F32),
        scratch_shapes=operands(n),
        cost_estimate=estimate(n, 10),
        compiler_params=pltpu.CompilerParams(vmem_limit_bytes=48 << 20),
    )(source, mine, inv)


def two_way(other, sides, inv):
    n = other.shape[1]
    count = len(sides)
    return pl.pallas_call(
        functools.partial(two_way_body, count=count),
        out_shape=(jax.ShapeDtypeStruct((17, n), F32),) * (count + 1),
        scratch_shapes=operands(n)
        + [
            pltpu.VMEM((48, n), BF16),
            pltpu.VMEM((64, n), LOW),
            pltpu.VMEM((48, n), F32),
            pltpu.VMEM((64, n), F32),
        ],
        cost_estimate=estimate(n, 20 * count),
        compiler_params=pltpu.CompilerParams(vmem_limit_bytes=48 << 20),
    )(other, *sides, inv)


AXES = ("blk", "half")


def near_pairs(blocks):
    return [((b ^ 1) * 2 + (h ^ (b & 1)), b * 2 + h) for b in range(blocks) for h in range(2)]


def hops(size, start, flip):
    away = ((start ^ flip) - start) % size
    ways = []
    if away and 2 * away <= size:
        ways.append((0, [(start + k) % size for k in range(away)], 0.5 if 2 * away == size else 1.0))
    if away and 2 * away >= size:
        ways.append((1, [(start - k) % size for k in range(size - away)], 0.5 if 2 * away == size else 1.0))
    return ways


RINGS = ((4, 5, 2), (8, 2, 3), (2, 1, 1))


def loads_of(mask, blocks):
    out = np.zeros((blocks, 3, 2, blocks), np.float32)
    for block in range(blocks):
        at = block
        for axis, (size, low, bits) in enumerate(RINGS):
            field = ((1 << bits) - 1) << low
            for way, places, share in hops(size, (at & field) >> low, (mask & field) >> low):
                for place in places:
                    out[block, axis, way, ((at & ~field) | (place << low)) & ~1] += share
            at = (at & ~field) | ((block ^ mask) & field)
    return out.reshape(blocks, -1)


def parity(x):
    return bin(x).count("1") & 1


def mate_routes(blocks):
    last = blocks - 1
    loads = {m: loads_of(m, blocks) for m in range(2, blocks)}
    kinds = np.array([[parity(w & b) for b in range(blocks)] for w in range(blocks)], np.float32)
    routes = []
    for mask in range(2, last):
        worst = (kinds @ (loads[last] - loads[mask]) + loads[mask].sum(0)).max(1)
        fits = [w for w in range(blocks) if parity(w & mask) and parity(w & last)]
        best = min(fits, key=lambda w: (float(worst[w]), w))
        routes.append(
            [(b * 2 + h, (b ^ (last if parity(best & b) else mask)) * 2 + h) for b in range(blocks) for h in range(2)]
        )
    return routes


def back(pairs):
    return [(b, a) for a, b in pairs]


def local(points, vectors, inv_length, signal_var, noise_var, masks):
    inv = (inv_length * STRETCH)[:, None]
    mine = jnp.concatenate([points, vectors], axis=0)
    blocks = lax.axis_size("blk")
    last = blocks - 1
    which = (masks[0] ^ masks[1] ^ masks[2] ^ 1 ^ last) - 2
    routes = mate_routes(blocks)
    neighbours = near_pairs(blocks)
    swap = [(0, 1), (1, 0)]

    near = lax.ppermute(mine, AXES, neighbours)
    sibling = lax.ppermute(mine, "half", swap)

    def fetch(route):
        def run(mine, inv):
            mate = lax.ppermute(mine, AXES, route)
            return mate, one_way(mine, mine, inv)

        return run

    def give(route):
        def run(par, sibling, mine, inv):
            returned = lax.ppermute(par, AXES, back(route))
            return returned, one_way(sibling, mine, inv)

        return run

    mate, own_self = lax.switch(which, [fetch(r) for r in routes], mine, inv)
    own_near, par_near = two_way(near, (mine,), inv)
    back_near = lax.ppermute(par_near, AXES, back(neighbours))
    own_mate, sibling_mate, par_mate = two_way(mate, (mine, sibling), inv)
    back_sibling = lax.ppermute(sibling_mate, "half", swap)
    back_mate, own_sibling = lax.switch(which, [give(r) for r in routes], par_mate, sibling, mine, inv)
    sums = own_self + own_sibling + own_near + own_mate + back_near + back_sibling + back_mate
    return (signal_var[0] * FACTOR) * sums + noise_var[0] * vectors


def solution(mesh):
    return jax.shard_map(
        local,
        mesh=mesh,
        in_specs=(P(None, AXES), P(None, AXES), P(), P(), P(), P()),
        out_specs=P(None, AXES),
        check_vma=False,
    )
```

```python
import functools
import math

import jax
import jax.numpy as jnp
import numpy as np
from jax import lax
from jax.experimental import pallas as pl
from jax.experimental.pallas import tpu as pltpu
from jax.sharding import PartitionSpec as P

F32 = jnp.float32
BF16 = jnp.bfloat16
LOW = jnp.float8_e5m2
LOG2E = math.log2(math.e)
ALPHA = 1.5 * LOG2E
BETA = 0.75 * LOG2E * LOG2E
FACTOR = math.exp(1.5) / (3.0 * LOG2E * LOG2E)
STRETCH = math.sqrt(5.0) * LOG2E
TINY = 1e-30
DEPTH = 256
COLUMNS = 256


def pieces(x, count):
    out = []
    for _ in range(count):
        part = x.astype(BF16).astype(F32)
        out.append(part)
        x = x - part
    return out


def features(points, inv):
    x = points * inv
    norm = jnp.sum(x * x, axis=0, keepdims=True)
    return pieces(x, 3), pieces(norm, 3)


def row_side(points, inv):
    (h, m, l), norm = features(points, inv)
    one = jnp.ones_like(norm[0])
    tail = jnp.concatenate(norm + [one, one, one], axis=0)
    rest = jnp.zeros((DEPTH - 198, points.shape[1]), F32)
    return jnp.concatenate([-2.0 * p for p in (h, h, m, h, l, m)] + [tail, rest], axis=0).astype(BF16)


def column_side(points, inv):
    (h, m, l), norm = features(points, inv)
    one = jnp.ones_like(norm[0])
    tail = jnp.concatenate([one, one, one] + norm, axis=0)
    rest = jnp.zeros((DEPTH - 198, points.shape[1]), F32)
    return jnp.concatenate([h, m, h, l, h, m, tail, rest], axis=0).astype(BF16)


def vector_side(vectors):
    pad = jnp.zeros((7, vectors.shape[1]), F32)
    hi, lo = pieces(vectors, 2)
    wide = jnp.concatenate([hi, pad, lo, pad], axis=0).astype(BF16)
    first = vectors.astype(LOW).astype(F32)
    second = vectors - first
    fill = jnp.zeros((16, vectors.shape[1]), F32)
    low = jnp.concatenate([first, pad, second, pad, fill], axis=0).astype(LOW)
    return wide, low


def kernel_values(squared):
    q = jnp.maximum(squared, TINY)
    h = -ALPHA - q * lax.rsqrt(q)
    values = (h * h + BETA) * jnp.exp2(h)
    hi = values.astype(BF16)
    return hi, (values - hi.astype(F32)).astype(LOW)


def dot(a, b):
    return jnp.dot(a, b, preferred_element_type=F32)


def dot_t(a, b):
    return lax.dot_general(a, b, (((1,), (1,)), ((), ())), preferred_element_type=F32)


def folded(wide, low):
    return wide[0:24] + wide[24:48] + low[0:24] + low[24:48]


def one_way_body(source, mine, inv, out, rows, cols, vec, vec_low):
    n = mine.shape[1]
    rows[...] = row_side(source[0:32, :], inv[...]).T
    cols[...] = column_side(mine[0:32, :], inv[...])
    vec[...], vec_low[...] = vector_side(source[32:49, :])

    def step(i, carry):
        c = pl.ds(pl.multiple_of(i * COLUMNS, COLUMNS), COLUMNS)
        hi, lo = kernel_values(dot(rows[...], cols[:, c]))
        out[:, c] = folded(dot(vec[...], hi), dot(vec_low[...], lo))[0:17]
        return carry

    lax.fori_loop(0, n // COLUMNS, step, 0)


def pairs_body(core, mine, sibling, beside, mate, inv, own, for_sibling, for_beside, for_mate, *scratch):
    rows, cols, vec_r, low_r, vec_c, low_c, acc, acc_low, par, total = scratch
    n = mine.shape[1]
    steps = n // COLUMNS
    for k, side in enumerate((mine, sibling)):
        rows[k] = row_side(side[0:32, :], inv[...]).T
        vec_r[k], low_r[k] = vector_side(side[32:49, :])
    for k, side in enumerate((beside, mate)):
        cols[k] = column_side(side[0:32, :], inv[...])
        vec_c[k], low_c[k] = vector_side(side[32:49, :])
    cols[2] = column_side(mine[0:32, :], inv[...])
    acc[...] = jnp.zeros_like(acc)
    acc_low[...] = jnp.zeros_like(acc_low)
    par[...] = jnp.zeros_like(par)

    def both(i, carry):
        tile = i // steps
        c = pl.ds(pl.multiple_of(lax.rem(i, steps) * COLUMNS, COLUMNS), COLUMNS)
        col = jnp.minimum(tile, 1)
        row = jnp.where(tile == 0, core[0], tile - 1)
        hi, lo = kernel_values(dot(rows[row], cols[col, :, c]))
        par[col, :, c] += folded(dot(vec_r[row], hi), dot(low_r[row], lo))
        acc[row] += dot_t(vec_c[col, :, c], hi)
        acc_low[row] += dot_t(low_c[col, :, c], lo)
        return carry

    lax.fori_loop(0, 3 * steps, both, 0)

    def one(i, carry):
        c = pl.ds(pl.multiple_of(i * COLUMNS, COLUMNS), COLUMNS)
        hi, lo = kernel_values(dot(rows[1], cols[2, :, c]))
        total[:, c] = folded(dot(vec_r[1], hi), dot(low_r[1], lo))
        return carry

    lax.fori_loop(0, steps, one, 0)
    own[...] = (total[...] + folded(acc[0], acc_low[0]))[0:17]
    for_sibling[...] = folded(acc[1], acc_low[1])[0:17]
    for_beside[...] = par[0, 0:17]
    for_mate[...] = par[1, 0:17]


def operands(n):
    return [
        pltpu.VMEM((n, DEPTH), BF16),
        pltpu.VMEM((DEPTH, n), BF16),
        pltpu.VMEM((48, n), BF16),
        pltpu.VMEM((64, n), LOW),
    ]


def estimate(n, passes):
    return pl.CostEstimate(flops=2 * n * n * 256 * passes, bytes_accessed=4 * 115 * n, transcendentals=2 * n * n)


def one_way(source, mine, inv):
    n = mine.shape[1]
    return pl.pallas_call(
        one_way_body,
        out_shape=jax.ShapeDtypeStruct((17, n), F32),
        scratch_shapes=operands(n),
        cost_estimate=estimate(n, 10),
        compiler_params=pltpu.CompilerParams(vmem_limit_bytes=48 << 20),
    )(source, mine, inv)


def pairs(core, mine, sibling, beside, mate, inv):
    n = mine.shape[1]
    whole = pl.BlockSpec(memory_space=pltpu.VMEM)
    return pl.pallas_call(
        pairs_body,
        out_shape=(jax.ShapeDtypeStruct((17, n), F32),) * 4,
        in_specs=[pl.BlockSpec(memory_space=pltpu.SMEM)] + [whole] * 5,
        scratch_shapes=[
            pltpu.VMEM((2, n, DEPTH), BF16),
            pltpu.VMEM((3, DEPTH, n), BF16),
            pltpu.VMEM((2, 48, n), BF16),
            pltpu.VMEM((2, 64, n), LOW),
            pltpu.VMEM((2, 48, n), BF16),
            pltpu.VMEM((2, 64, n), LOW),
            pltpu.VMEM((2, 48, n), F32),
            pltpu.VMEM((2, 64, n), F32),
            pltpu.VMEM((2, 24, n), F32),
            pltpu.VMEM((24, n), F32),
        ],
        cost_estimate=estimate(n, 70),
        compiler_params=pltpu.CompilerParams(vmem_limit_bytes=48 << 20),
    )(core, mine, sibling, beside, mate, inv)


AXES = ("blk", "half")
MESH = pl.DeviceIdType.MESH


def exchange_body(source, target, sems, *, route, forth):
    mask, last, kind = route
    block, half = lax.axis_index("blk"), lax.axis_index("half")
    bits = {k: lax.rem(lax.div(block, 1 << k), 2) for k in range(last.bit_length()) if (mask | kind) >> k & 1}
    one = block + mask - sum(bits[k] * (2 << k) for k in bits if mask >> k & 1)
    two = last - block
    change = lax.rem(sum(bits[k] for k in bits if kind >> k & 1), 2) * (two - one)
    ways = one + change, two - change
    to, sender = ways if forth else ways[::-1]
    barrier = pltpu.get_barrier_semaphore()
    pl.semaphore_signal(barrier, inc=1, device_id=(sender, half), device_id_type=MESH)
    pl.semaphore_wait(barrier, 1)
    copy = pltpu.make_async_remote_copy(
        src_ref=source,
        dst_ref=target,
        send_sem=sems.at[0],
        recv_sem=sems.at[1],
        device_id=(to, half),
        device_id_type=MESH,
    )
    copy.start()
    copy.wait()


def exchange(source, route, forth, number):
    hbm = pl.BlockSpec(memory_space=pl.ANY)
    return pl.pallas_call(
        functools.partial(exchange_body, route=route, forth=forth),
        out_shape=jax.ShapeDtypeStruct(source.shape, F32),
        in_specs=[hbm],
        out_specs=hbm,
        scratch_shapes=[pltpu.SemaphoreType.DMA((2,))],
        compiler_params=pltpu.CompilerParams(collective_id=number, has_side_effects=True),
    )(source)


def hops(size, start, flip):
    away = ((start ^ flip) - start) % size
    ways = []
    if away and 2 * away <= size:
        ways.append((0, [(start + k) % size for k in range(away)], 0.5 if 2 * away == size else 1.0))
    if away and 2 * away >= size:
        ways.append((1, [(start - k) % size for k in range(size - away)], 0.5 if 2 * away == size else 1.0))
    return ways


RINGS = ((4, 5, 2), (8, 2, 3), (2, 1, 1))


def loads_of(mask, blocks):
    out = np.zeros((blocks, 3, 2, blocks), np.float32)
    for block in range(blocks):
        at = block
        for axis, (size, low, bits) in enumerate(RINGS):
            field = ((1 << bits) - 1) << low
            for way, places, share in hops(size, (at & field) >> low, (mask & field) >> low):
                for place in places:
                    out[block, axis, way, ((at & ~field) | (place << low)) & ~1] += share
            at = (at & ~field) | ((block ^ mask) & field)
    return out.reshape(blocks, -1)


def parity(x):
    return bin(x).count("1") & 1


def mate_routes(blocks):
    last = blocks - 1
    loads = {m: loads_of(m, blocks) for m in [*range(2, blocks, 2), last]}
    kinds = np.array([[parity(w & b) for b in range(blocks)] for w in range(blocks)], np.float32)
    routes = []
    for mask in range(2, last, 2):
        worst = (kinds @ (loads[last] - loads[mask]) + loads[mask].sum(0)).max(1)
        fits = [w for w in range(0, blocks, 2) if parity(w & mask) and parity(w & last)]
        best = min(fits, key=lambda w: (round(float(worst[w]), 3), bin(w).count(str(1)), w))
        routes.append((mask, last, best))
    return routes


def local(points, vectors, inv_length, signal_var, noise_var, masks):
    inv = (inv_length * STRETCH)[:, None]
    mine = jnp.concatenate([points, vectors], axis=0)
    blocks = lax.axis_size("blk")
    last = blocks - 1
    middle = masks[0] ^ masks[1] ^ masks[2] ^ 1 ^ last
    which = (middle >> 1) - 1
    routes = mate_routes(blocks)
    kinds = jnp.array([r[2] for r in routes], jnp.int32)
    block = lax.axis_index("blk")
    core = block & 1
    kind = lax.population_count(kinds[which] & block) & 1
    lent = (kind == 0) & (middle & 1 == 1)

    chip = [(b, b ^ 1) for b in range(blocks)]
    swap = [(0, 1), (1, 0)]
    beside = lax.ppermute(mine, "blk", chip)
    sibling = lax.ppermute(mine, "half", swap)
    own_self = one_way(mine, mine, inv)
    sent = jnp.where(lent, beside, mine)
    mate = lax.switch(
        which, [functools.partial(exchange, route=r, forth=True, number=2 * k) for k, r in enumerate(routes)], sent
    )
    own, for_sibling, for_beside, for_mate = pairs(core.reshape(1), mine, sibling, beside, mate, inv)
    from_sibling = lax.ppermute(for_sibling, "half", swap)
    returned = lax.switch(
        which,
        [functools.partial(exchange, route=r, forth=False, number=2 * k + 1) for k, r in enumerate(routes)],
        for_mate,
    )
    from_beside = lax.ppermute(for_beside + jnp.where(lent, returned, 0.0), "blk", chip)
    sums = own_self + own + from_sibling + from_beside + jnp.where(lent, 0.0, returned)
    return (signal_var[0] * FACTOR) * sums + noise_var[0] * vectors


def solution(mesh):
    return jax.shard_map(
        local,
        mesh=mesh,
        in_specs=(P(None, AXES), P(None, AXES), P(), P(), P(), P()),
        out_specs=P(None, AXES),
        check_vma=False,
    )
```

```python
import functools
import math

import jax
import jax.numpy as jnp
import numpy as np
from jax import lax
from jax.experimental import pallas as pl
from jax.experimental.pallas import tpu as pltpu
from jax.sharding import PartitionSpec as P

F32 = jnp.float32
BF16 = jnp.bfloat16
LOW = jnp.float8_e5m2
LOG2E = math.log2(math.e)
ALPHA = 1.5 * LOG2E
BETA = 0.75 * LOG2E * LOG2E
FACTOR = math.exp(1.5) / (3.0 * LOG2E * LOG2E)
STRETCH = math.sqrt(5.0) * LOG2E
TINY = 1e-30
DEPTH = 256
COLUMNS = 256


def pieces(x, count):
    out = []
    for _ in range(count):
        part = x.astype(BF16).astype(F32)
        out.append(part)
        x = x - part
    return out


def features(points, inv):
    x = points * inv
    norm = jnp.sum(x * x, axis=0, keepdims=True)
    return pieces(x, 3), pieces(norm, 3)


def row_side(points, inv):
    (h, m, l), norm = features(points, inv)
    one = jnp.ones_like(norm[0])
    tail = jnp.concatenate(norm + [one, one, one], axis=0)
    rest = jnp.zeros((DEPTH - 198, points.shape[1]), F32)
    return jnp.concatenate([-2.0 * p for p in (h, h, m, h, l, m)] + [tail, rest], axis=0).astype(BF16)


def column_side(points, inv):
    (h, m, l), norm = features(points, inv)
    one = jnp.ones_like(norm[0])
    tail = jnp.concatenate([one, one, one] + norm, axis=0)
    rest = jnp.zeros((DEPTH - 198, points.shape[1]), F32)
    return jnp.concatenate([h, m, h, l, h, m, tail, rest], axis=0).astype(BF16)


def vector_side(vectors):
    pad = jnp.zeros((7, vectors.shape[1]), F32)
    hi, lo = pieces(vectors, 2)
    wide = jnp.concatenate([hi, pad, lo, pad], axis=0).astype(BF16)
    first = vectors.astype(LOW).astype(F32)
    second = vectors - first
    fill = jnp.zeros((16, vectors.shape[1]), F32)
    low = jnp.concatenate([first, pad, second, pad, fill], axis=0).astype(LOW)
    return wide, low


def kernel_values(squared):
    q = jnp.maximum(squared, TINY)
    h = -ALPHA - q * lax.rsqrt(q)
    values = (h * h + BETA) * jnp.exp2(h)
    hi = values.astype(BF16)
    return hi, (values - hi.astype(F32)).astype(LOW)


def dot(a, b):
    return jnp.dot(a, b, preferred_element_type=F32)


def dot_t(a, b):
    return lax.dot_general(a, b, (((1,), (1,)), ((), ())), preferred_element_type=F32)


def folded(wide, low):
    return wide[0:24] + wide[24:48] + low[0:24] + low[24:48]


def column_step(i):
    return pl.ds(pl.multiple_of(i * COLUMNS, COLUMNS), COLUMNS)


def by_columns(n, step):
    def run(i, carry):
        step(pl.ds(pl.multiple_of(i * COLUMNS, COLUMNS), COLUMNS))
        return carry

    lax.fori_loop(0, n // COLUMNS, run, 0)


def one_way_body(source, mine, inv, base, out, rows, cols, vec, vec_low):
    n = mine.shape[1]

    def prepare(c):
        rows[c, :] = row_side(source[0:32, c], inv[...]).T
        cols[:, c] = column_side(mine[0:32, c], inv[...])
        vec[:, c], vec_low[:, c] = vector_side(source[32:49, c])

    def step(c):
        hi, lo = kernel_values(dot(rows[...], cols[:, c]))
        out[:, c] = base[:, c] + folded(dot(vec[...], hi), dot(vec_low[...], lo))[0:17]

    by_columns(n, prepare)
    by_columns(n, step)


def two_way_body(core, mine, sibling, other, inv, near, base, own, for_sibling, par, *scratch, count):
    rows, cols, vec_r, low_r, vec_c, low_c, acc, acc_low = scratch
    n = mine.shape[1]
    par[...] = jnp.zeros_like(par)

    def prepare_columns(c):
        cols[:, c] = column_side(other[0:32, c], inv[...])
        vec_c[:, c], low_c[:, c] = vector_side(other[32:49, c])

    by_columns(n, prepare_columns)

    def tile(k, carry):
        second = (core[0] if count == 1 else k) == 1

        def prepare_rows(c):
            side = jnp.where(second, sibling[:, c], mine[:, c])
            rows[c, :] = row_side(side[0:32, :], inv[...]).T
            vec_r[:, c], low_r[:, c] = vector_side(side[32:49, :])

        def step(c):
            hi, lo = kernel_values(dot(rows[...], cols[:, c]))
            par[:, c] += folded(dot(vec_r[...], hi), dot(low_r[...], lo))[0:17]
            acc[...] += dot_t(vec_c[:, c], hi)
            acc_low[...] += dot_t(low_c[:, c], lo)

        by_columns(n, prepare_rows)
        acc[...] = jnp.zeros_like(acc)
        acc_low[...] = jnp.zeros_like(acc_low)
        by_columns(n, step)
        total = folded(acc[...], acc_low[...])[0:17]
        if count == 1:
            own[...] = base[...] + jnp.where(second, 0.0, total)
            for_sibling[...] = near[...] + jnp.where(second, total, 0.0)
        else:

            @pl.when(k == 0)
            def _():
                own[...] = base[...] + total

            @pl.when(k == 1)
            def _():
                for_sibling[...] = near[...] + total

        return carry

    lax.fori_loop(0, count, tile, 0)


def operands(n):
    return [
        pltpu.VMEM((n, DEPTH), BF16),
        pltpu.VMEM((DEPTH, n), BF16),
        pltpu.VMEM((48, n), BF16),
        pltpu.VMEM((64, n), LOW),
    ]


def estimate(n, passes):
    return pl.CostEstimate(flops=2 * n * n * 256 * passes, bytes_accessed=4 * 115 * n, transcendentals=2 * n * n)


def tile_call(body, outs, passes, core, *arrays):
    n = arrays[0].shape[1]
    whole = pl.BlockSpec(memory_space=pltpu.VMEM)
    scratch = operands(n)
    if core is not None:
        scratch += [
            pltpu.VMEM((48, n), BF16),
            pltpu.VMEM((64, n), LOW),
            pltpu.VMEM((48, n), F32),
            pltpu.VMEM((64, n), F32),
        ]
        arrays = (core,) + arrays
    specs = [whole] * len(arrays)
    if core is not None:
        specs[0] = pl.BlockSpec(memory_space=pltpu.SMEM)
    return pl.pallas_call(
        body,
        out_shape=(jax.ShapeDtypeStruct((17, n), F32),) * outs,
        in_specs=specs,
        scratch_shapes=scratch,
        cost_estimate=estimate(n, passes),
        compiler_params=pltpu.CompilerParams(vmem_limit_bytes=48 << 20),
    )(*arrays)


AXES = ("blk", "half")
MESH = pl.DeviceIdType.MESH


def exchange_body(there, back, got, returned, sems, *, route):
    mask, last, kind = route
    block, half = lax.axis_index("blk"), lax.axis_index("half")
    bits = {k: lax.rem(lax.div(block, 1 << k), 2) for k in range(last.bit_length()) if (mask | kind) >> k & 1}
    one = block + mask - sum(bits[k] * (2 << k) for k in bits if mask >> k & 1)
    two = last - block
    change = lax.rem(sum(bits[k] for k in bits if kind >> k & 1), 2) * (two - one)
    ways = (one + change, half), (two - change, half)
    barrier = pltpu.get_barrier_semaphore()
    for device in ways:
        pl.semaphore_signal(barrier, inc=1, device_id=device, device_id_type=MESH)
    pl.semaphore_wait(barrier, 2)
    copies = [
        pltpu.make_async_remote_copy(
            src_ref=source,
            dst_ref=target,
            send_sem=sems.at[0, k],
            recv_sem=sems.at[1, k],
            device_id=device,
            device_id_type=MESH,
        )
        for k, (source, target, device) in enumerate(((there, got, ways[0]), (back, returned, ways[1])))
    ]
    for copy in copies:
        copy.start()
    for copy in copies:
        copy.wait()


def exchange(there, back, route, number):
    hbm = pl.BlockSpec(memory_space=pl.ANY)
    return pl.pallas_call(
        functools.partial(exchange_body, route=route),
        out_shape=(jax.ShapeDtypeStruct(there.shape, F32), jax.ShapeDtypeStruct(back.shape, F32)),
        in_specs=[hbm] * 2,
        out_specs=(hbm,) * 2,
        scratch_shapes=[pltpu.SemaphoreType.DMA((2, 2))],
        compiler_params=pltpu.CompilerParams(collective_id=number, has_side_effects=True),
    )(there, back)


def hops(size, start, flip):
    away = ((start ^ flip) - start) % size
    ways = []
    if away and 2 * away <= size:
        ways.append((0, [(start + k) % size for k in range(away)], 0.5 if 2 * away == size else 1.0))
    if away and 2 * away >= size:
        ways.append((1, [(start - k) % size for k in range(size - away)], 0.5 if 2 * away == size else 1.0))
    return ways


RINGS = ((4, 5, 2), (8, 2, 3), (2, 1, 1))


def loads_of(mask, blocks):
    out = np.zeros((blocks, 3, 2, blocks), np.float32)
    for block in range(blocks):
        at = block
        for axis, (size, low, bits) in enumerate(RINGS):
            field = ((1 << bits) - 1) << low
            for way, places, share in hops(size, (at & field) >> low, (mask & field) >> low):
                for place in places:
                    out[block, axis, way, ((at & ~field) | (place << low)) & ~1] += share
            at = (at & ~field) | ((block ^ mask) & field)
    return out.reshape(blocks, -1)


def parity(x):
    return bin(x).count("1") & 1


def mate_routes(blocks):
    last = blocks - 1
    masks = range(4, blocks, 4)
    loads = {m: loads_of(m, blocks) for m in [*masks, last]}
    kinds = np.array([[parity(w & b) for b in range(blocks)] for w in range(blocks)], np.float32)
    routes = [(2, last, 2)]
    for mask in masks:
        worst = (kinds @ (loads[last] - loads[mask]) + loads[mask].sum(0)).max(1)
        fits = [w for w in range(0, blocks, 4) if parity(w & mask) and parity(w & last)]
        best = min(fits, key=lambda w: (round(float(worst[w]), 3), bin(w).count(str(1)), w))
        routes.append((mask, last, best))
    return routes


def local(points, vectors, inv_length, signal_var, noise_var, masks):
    inv = (inv_length * STRETCH)[:, None]
    mine = jnp.concatenate([points, vectors], axis=0)
    blocks = lax.axis_size("blk")
    last = blocks - 1
    middle = masks[0] ^ masks[1] ^ masks[2] ^ 1 ^ last
    which = middle >> 2
    routes = mate_routes(blocks)
    block = lax.axis_index("blk")
    core = (block & 1).reshape(1)
    kind = jnp.int32(0)
    for k in range(last.bit_length()):
        having = sum(1 << i for i, r in enumerate(routes) if r[2] >> k & 1)
        kind = kind ^ (np.uint32(having).astype(np.int32) >> which & block >> k & 1)
    lends = kind == 0
    lent_chip = lends & (middle & 1 == 1)
    lent_far = lends & (middle & 2 == 2) & (which > 0)

    chip = [(b, b ^ 1) for b in range(blocks)]
    apart = [(b, b ^ 2) for b in range(blocks)]
    swap = [(0, 1), (1, 0)]
    beside = lax.ppermute(mine, "blk", chip)
    sibling = lax.ppermute(mine, "half", swap)
    (own_self,) = tile_call(one_way_body, 1, 10, None, mine, mine, inv, jnp.zeros_like(vectors))
    beside, own_self = lax.optimization_barrier((beside, own_self))
    lent = jnp.where(lent_chip, beside, mine)
    across = lax.ppermute(lent, "blk", apart)
    zero = jnp.zeros_like(vectors)
    own, for_sibling, for_beside = tile_call(
        functools.partial(two_way_body, count=1), 3, 20, core, mine, sibling, beside, inv, zero, own_self
    )
    across, own = lax.optimization_barrier((across, own))
    sent = jnp.where(lent_far, across, lent)

    ways = [functools.partial(exchange, route=r, number=k) for k, r in enumerate(routes)]
    mate, _ = lax.switch(which, ways, sent, vectors)
    own, for_sibling, for_mate = tile_call(
        functools.partial(two_way_body, count=2), 3, 40, core, mine, sibling, mate, inv, for_sibling, own
    )
    from_sibling = lax.ppermute(for_sibling, "half", swap)
    _, returned = lax.switch(which, ways, mate, for_mate)
    from_across = lax.ppermute(jnp.where(lent_far, returned, 0.0), "blk", apart)
    (own,) = tile_call(one_way_body, 1, 10, None, sibling, mine, inv, own)
    kept = jnp.where(lent_far, 0.0, returned) + from_across
    from_beside = lax.ppermute(for_beside + jnp.where(lent_chip, kept, 0.0), "blk", chip)
    sums = own + from_sibling + from_beside + jnp.where(lent_chip, 0.0, kept)
    return (signal_var[0] * FACTOR) * sums + noise_var[0] * vectors


def solution(mesh):
    return jax.shard_map(
        local,
        mesh=mesh,
        in_specs=(P(None, AXES), P(None, AXES), P(), P(), P(), P()),
        out_specs=P(None, AXES),
        check_vma=False,
    )
```

```python
import functools
import math

import jax
import jax.numpy as jnp
import numpy as np
from jax import lax
from jax.experimental import pallas as pl
from jax.experimental.pallas import tpu as pltpu
from jax.sharding import PartitionSpec as P

F32 = jnp.float32
BF16 = jnp.bfloat16
LOW = jnp.float8_e5m2
LOG2E = math.log2(math.e)
ALPHA = 1.5 * LOG2E
BETA = 0.75 * LOG2E * LOG2E
FACTOR = math.exp(1.5) / (3.0 * LOG2E * LOG2E)
STRETCH = math.sqrt(5.0) * LOG2E
TINY = 1e-30
DEPTH = 256
COLUMNS = 256
ROWS = 768


def pieces(x, count):
    out = []
    for _ in range(count):
        part = x.astype(BF16).astype(F32)
        out.append(part)
        x = x - part
    return out


def features(points, inv):
    x = points * inv
    norm = jnp.sum(x * x, axis=0, keepdims=True)
    return pieces(x, 3), pieces(norm, 3)


def row_side(points, inv):
    (h, m, l), norm = features(points, inv)
    one = jnp.ones_like(norm[0])
    tail = jnp.concatenate(norm + [one, one, one], axis=0)
    rest = jnp.zeros((DEPTH - 198, points.shape[1]), F32)
    return jnp.concatenate([-2.0 * p for p in (h, h, m, h, l, m)] + [tail, rest], axis=0).astype(BF16)


def column_side(points, inv):
    (h, m, l), norm = features(points, inv)
    one = jnp.ones_like(norm[0])
    tail = jnp.concatenate([one, one, one] + norm, axis=0)
    rest = jnp.zeros((DEPTH - 198, points.shape[1]), F32)
    return jnp.concatenate([h, m, h, l, h, m, tail, rest], axis=0).astype(BF16)


def vector_side(vectors):
    pad = jnp.zeros((7, vectors.shape[1]), F32)
    hi, lo = pieces(vectors, 2)
    wide = jnp.concatenate([hi, pad, lo, pad], axis=0).astype(BF16)
    first = vectors.astype(LOW).astype(F32)
    second = vectors - first
    fill = jnp.zeros((16, vectors.shape[1]), F32)
    low = jnp.concatenate([first, pad, second, pad, fill], axis=0).astype(LOW)
    return wide, low


def kernel_values(squared):
    q = jnp.maximum(squared, TINY)
    h = -ALPHA - q * lax.rsqrt(q)
    values = (h * h + BETA) * jnp.exp2(h)
    hi = values.astype(BF16)
    return hi, (values - hi.astype(F32)).astype(LOW)


def dot(a, b):
    return jnp.dot(a, b, preferred_element_type=F32)


def dot_t(a, b):
    return lax.dot_general(a, b, (((1,), (1,)), ((), ())), preferred_element_type=F32)


def folded(wide, low):
    return wide[0:24] + wide[24:48] + low[0:24] + low[24:48]


def column_step(i):
    return pl.ds(pl.multiple_of(i * COLUMNS, COLUMNS), COLUMNS)


def by_columns(n, step):
    def run(i, carry):
        step(pl.ds(pl.multiple_of(i * COLUMNS, COLUMNS), COLUMNS))
        return carry

    lax.fori_loop(0, n // COLUMNS, run, 0)


def one_way_body(source, mine, inv, base, *refs):
    before, (out, rows, vec, low, cols) = refs[:-5], refs[-5:]
    n = mine.shape[1]
    at = rows.shape[0] - 1

    def prepare(c):
        if before:
            rows[0, c, :] = before[0][0, c, :]
            vec[0, :, c], low[0, :, c] = before[1][0, :, c], before[2][0, :, c]
        rows[at, c, :] = row_side(source[0:32, c], inv[...]).T
        vec[at, :, c], low[at, :, c] = vector_side(source[32:49, c])
        cols[:, c] = column_side(mine[0:32, c], inv[...])

    def step(c):
        hi, lo = kernel_values(dot(rows[at], cols[:, c]))
        out[:, c] = base[:, c] + folded(dot(vec[at], hi), dot(low[at], lo))[0:17]

    by_columns(n, prepare)
    by_columns(n, step)


def estimate(n, passes):
    return pl.CostEstimate(flops=2 * n * n * 256 * passes, bytes_accessed=4 * 115 * n, transcendentals=2 * n * n)


def one_way(source, mine, inv, base, before=()):
    n = mine.shape[1]
    halves = 2 if before else 1
    return pl.pallas_call(
        one_way_body,
        out_shape=(
            jax.ShapeDtypeStruct((17, n), F32),
            jax.ShapeDtypeStruct((halves, n, DEPTH), BF16),
            jax.ShapeDtypeStruct((halves, 48, n), BF16),
            jax.ShapeDtypeStruct((halves, 64, n), LOW),
        ),
        scratch_shapes=[pltpu.VMEM((DEPTH, n), BF16)],
        cost_estimate=estimate(n, 10),
        compiler_params=pltpu.CompilerParams(vmem_limit_bytes=48 << 20),
    )(source, mine, inv, base, *before)


AXES = ("blk", "half")
MESH = pl.DeviceIdType.MESH


def rounds_body(
    sent, beside, inv, base, rows, vec_r, low_r, own, for_sibling, for_beside, returned, *scratch, route
):
    land, cols, vec_c, low_c, acc, acc_low, par, back, sems, back_sems = scratch
    n = beside.shape[1]
    parts = n // ROWS
    steps = n // COLUMNS
    mask, last, kind = route
    block, half = lax.axis_index("blk"), lax.axis_index("half")
    core = lax.rem(block, 2)
    bits = {k: lax.rem(lax.div(block, 1 << k), 2) for k in range(last.bit_length()) if (mask | kind) >> k & 1}
    one = block + mask - sum(bits[k] * (2 << k) for k in bits if mask >> k & 1)
    two = last - block
    change = lax.rem(sum(bits[k] for k in bits if kind >> k & 1), 2) * (two - one)
    to, sender = (one + change, half), (two - change, half)

    barrier = pltpu.get_barrier_semaphore()
    for device in (to, sender):
        pl.semaphore_signal(barrier, inc=1, device_id=device, device_id_type=MESH)
    pl.semaphore_wait(barrier, 2)
    fetch = pltpu.make_async_remote_copy(
        src_ref=sent,
        dst_ref=land.at[1],
        send_sem=sems.at[0],
        recv_sem=sems.at[1],
        device_id=to,
        device_id_type=MESH,
    )
    fetch.start()

    def give(i):
        c = pl.ds(pl.multiple_of(i * COLUMNS, COLUMNS), COLUMNS)
        return pltpu.make_async_remote_copy(
            src_ref=par.at[1, :, c],
            dst_ref=back.at[:, c],
            send_sem=back_sems.at[0, i],
            recv_sem=back_sems.at[1, i],
            device_id=sender,
            device_id_type=MESH,
        )

    def clear(c):
        land[0, :, c] = beside[:, c]
        acc[:, :, c] = jnp.zeros((2, 48, COLUMNS), F32)
        acc_low[:, :, c] = jnp.zeros((2, 64, COLUMNS), F32)
        par[:, :, c] = jnp.zeros((2, 24, COLUMNS), F32)

    by_columns(n, clear)

    first = steps * parts

    def tile(i, carry):
        late = lax.div(lax.div(i, first) + 1, 2)
        left = i - late * first
        visits = (1 + late) * parts
        at = lax.div(left, visits)
        visit = lax.rem(left, visits)
        row = (1 - late) * core + late * lax.div(visit, parts)
        c = pl.ds(pl.multiple_of(at * COLUMNS, COLUMNS), COLUMNS)
        r = pl.ds(pl.multiple_of(lax.rem(visit, parts) * ROWS, ROWS), ROWS)

        @pl.when(i == first)
        def _():
            fetch.wait()

        @pl.when(visit == 0)
        def _():
            other = land[late, :, c]
            cols[...] = column_side(other[0:32, :], inv[...])
            vec_c[...], low_c[...] = vector_side(other[32:49, :])

        hi, lo = kernel_values(dot(rows[row, r, :], cols[...]))
        par[late, :, c] += folded(dot(vec_r[row, :, r], hi), dot(low_r[row, :, r], lo))
        acc[row, :, r] += dot_t(vec_c[...], hi)
        acc_low[row, :, r] += dot_t(low_c[...], lo)

        @pl.when(late * visit == 2 * parts - 1)
        def _():
            give(at).start()

        return carry

    lax.fori_loop(0, 3 * first, tile, 0)

    def total(c):
        own[:, c] = base[:, c] + folded(acc[0, :, c], acc_low[0, :, c])[0:17]
        for_sibling[:, c] = folded(acc[1, :, c], acc_low[1, :, c])[0:17]
        for_beside[:, c] = par[0, 0:17, c]

    def finish(i, carry):
        give(i).wait()
        c = pl.ds(pl.multiple_of(i * COLUMNS, COLUMNS), COLUMNS)
        returned[:, c] = back[0:17, c]
        return carry

    by_columns(n, total)
    lax.fori_loop(0, steps, finish, 0)


def rounds(sent, beside, inv, base, rows, vec, low, route, number):
    n = beside.shape[1]
    steps = n // COLUMNS
    whole = pl.BlockSpec(memory_space=pltpu.VMEM)
    return pl.pallas_call(
        functools.partial(rounds_body, route=route),
        out_shape=(jax.ShapeDtypeStruct((17, n), F32),) * 4,
        in_specs=[whole] * 7,
        out_specs=(whole,) * 4,
        scratch_shapes=[
            pltpu.VMEM((2, 49, n), F32),
            pltpu.VMEM((DEPTH, COLUMNS), BF16),
            pltpu.VMEM((48, COLUMNS), BF16),
            pltpu.VMEM((64, COLUMNS), LOW),
            pltpu.VMEM((2, 48, n), F32),
            pltpu.VMEM((2, 64, n), F32),
            pltpu.VMEM((2, 24, n), F32),
            pltpu.VMEM((24, n), F32),
            pltpu.SemaphoreType.DMA((2,)),
            pltpu.SemaphoreType.DMA((2, steps)),
        ],
        cost_estimate=estimate(n, 60),
        compiler_params=pltpu.CompilerParams(
            collective_id=number, has_side_effects=True, vmem_limit_bytes=48 << 20
        ),
    )(sent, beside, inv, base, rows, vec, low)


def hops(size, start, flip):
    away = ((start ^ flip) - start) % size
    ways = []
    if away and 2 * away <= size:
        ways.append((0, [(start + k) % size for k in range(away)], 0.5 if 2 * away == size else 1.0))
    if away and 2 * away >= size:
        ways.append((1, [(start - k) % size for k in range(size - away)], 0.5 if 2 * away == size else 1.0))
    return ways


RINGS = ((4, 5, 2), (8, 2, 3), (2, 1, 1))


def loads_of(mask, blocks):
    out = np.zeros((blocks, 3, 2, blocks), np.float32)
    for block in range(blocks):
        at = block
        for axis, (size, low, bits) in enumerate(RINGS):
            field = ((1 << bits) - 1) << low
            for way, places, share in hops(size, (at & field) >> low, (mask & field) >> low):
                for place in places:
                    out[block, axis, way, ((at & ~field) | (place << low)) & ~1] += share
            at = (at & ~field) | ((block ^ mask) & field)
    return out.reshape(blocks, -1)


def parity(x):
    return bin(x).count("1") & 1


def mate_routes(blocks):
    last = blocks - 1
    masks = range(4, blocks, 4)
    loads = {m: loads_of(m, blocks) for m in [*masks, last]}
    kinds = np.array([[parity(w & b) for b in range(blocks)] for w in range(blocks)], np.float32)
    routes = [(2, last, 2)]
    for mask in masks:
        worst = (kinds @ (loads[last] - loads[mask]) + loads[mask].sum(0)).max(1)
        fits = [w for w in range(0, blocks, 4) if parity(w & mask) and parity(w & last)]
        best = min(fits, key=lambda w: (round(float(worst[w]), 3), bin(w).count(str(1)), w))
        routes.append((mask, last, best))
    return routes


def local(points, vectors, inv_length, signal_var, noise_var, masks):
    inv = (inv_length * STRETCH)[:, None]
    mine = jnp.concatenate([points, vectors], axis=0)
    blocks = lax.axis_size("blk")
    last = blocks - 1
    middle = masks[0] ^ masks[1] ^ masks[2] ^ 1 ^ last
    which = middle >> 2
    routes = mate_routes(blocks)
    block = lax.axis_index("blk")
    kind = jnp.int32(0)
    for k in range(last.bit_length()):
        having = sum(1 << i for i, r in enumerate(routes) if r[2] >> k & 1)
        kind = kind ^ (np.uint32(having).astype(np.int32) >> which & block >> k & 1)
    lends = kind == 0
    lent_chip = lends & (middle & 1 == 1)
    lent_far = lends & (middle & 2 == 2) & (which > 0)

    chip = [(b, b ^ 1) for b in range(blocks)]
    apart = [(b, b ^ 2) for b in range(blocks)]
    swap = [(0, 1), (1, 0)]
    beside = lax.ppermute(mine, "blk", chip)
    sibling = lax.ppermute(mine, "half", swap)
    own, *before = one_way(mine, mine, inv, jnp.zeros_like(vectors))
    beside, own = lax.optimization_barrier((beside, own))
    lent = jnp.where(lent_chip, beside, mine)
    across = lax.ppermute(lent, "blk", apart)
    own, *rows = one_way(sibling, mine, inv, own, before)
    across, own = lax.optimization_barrier((across, own))
    sent = jnp.where(lent_far, across, lent)
    ways = [functools.partial(rounds, route=r, number=k) for k, r in enumerate(routes)]
    own, for_sibling, for_beside, returned = lax.switch(which, ways, sent, beside, inv, own, *rows)
    from_sibling = lax.ppermute(for_sibling, "half", swap)
    from_across = lax.ppermute(jnp.where(lent_far, returned, 0.0), "blk", apart)
    kept = jnp.where(lent_far, 0.0, returned) + from_across
    from_beside = lax.ppermute(for_beside + jnp.where(lent_chip, kept, 0.0), "blk", chip)
    sums = own + from_sibling + from_beside + jnp.where(lent_chip, 0.0, kept)
    return (signal_var[0] * FACTOR) * sums + noise_var[0] * vectors


def solution(mesh):
    return jax.shard_map(
        local,
        mesh=mesh,
        in_specs=(P(None, AXES), P(None, AXES), P(), P(), P(), P()),
        out_specs=P(None, AXES),
        check_vma=False,
    )
```

```python
import functools
import math

import jax
import jax.numpy as jnp
import numpy as np
from jax import lax
from jax.experimental import pallas as pl
from jax.experimental.pallas import tpu as pltpu
from jax.sharding import PartitionSpec as P

F32 = jnp.float32
BF16 = jnp.bfloat16
LOW = jnp.float8_e5m2
LOG2E = math.log2(math.e)
ALPHA = 1.5 * LOG2E
BETA = 0.75 * LOG2E * LOG2E
FACTOR = math.exp(1.5) / (3.0 * LOG2E * LOG2E)
STRETCH = math.sqrt(5.0) * LOG2E
TINY = 1e-30
DEPTH = 256
COLUMNS = 256
ROWS = 512
FAR = 1e30


def pieces(x, count):
    out = []
    for _ in range(count):
        part = x.astype(BF16).astype(F32)
        out.append(part)
        x = x - part
    return out


def features(points, inv):
    x = points * inv
    norm = jnp.sum(x * x, axis=0, keepdims=True)
    return pieces(x, 3), pieces(norm, 3)


def row_side(points, inv):
    (h, m, l), norm = features(points, inv)
    one = jnp.ones_like(norm[0])
    tail = jnp.concatenate(norm + [one, one, one], axis=0)
    rest = jnp.zeros((DEPTH - 198, points.shape[1]), F32)
    return jnp.concatenate([-2.0 * p for p in (h, h, m, h, l, m)] + [tail, rest], axis=0).astype(BF16)


def column_side(points, inv):
    (h, m, l), norm = features(points, inv)
    one = jnp.ones_like(norm[0])
    tail = jnp.concatenate([one, one, one] + norm, axis=0)
    rest = jnp.zeros((DEPTH - 198, points.shape[1]), F32)
    return jnp.concatenate([h, m, h, l, h, m, tail, rest], axis=0).astype(BF16)


def vector_side(vectors):
    pad = jnp.zeros((7, vectors.shape[1]), F32)
    hi, lo = pieces(vectors, 2)
    wide = jnp.concatenate([hi, pad, lo, pad], axis=0).astype(BF16)
    first = vectors.astype(LOW).astype(F32)
    second = vectors - first
    fill = jnp.zeros((16, vectors.shape[1]), F32)
    low = jnp.concatenate([first, pad, second, pad, fill], axis=0).astype(LOW)
    return wide, low


def kernel_values(squared):
    q = jnp.maximum(squared, TINY)
    h = -ALPHA - q * lax.rsqrt(q)
    values = (h * h + BETA) * jnp.exp2(h)
    hi = values.astype(BF16)
    return hi, (values - hi.astype(F32)).astype(LOW)


def dot(a, b):
    return jnp.dot(a, b, preferred_element_type=F32)


def dot_t(a, b):
    return lax.dot_general(a, b, (((1,), (1,)), ((), ())), preferred_element_type=F32)


def folded(wide, low):
    return wide[0:24] + wide[24:48] + low[0:24] + low[24:48]


def column_step(i):
    return pl.ds(pl.multiple_of(i * COLUMNS, COLUMNS), COLUMNS)


def column_step(i):
    return pl.ds(pl.multiple_of(i * COLUMNS, COLUMNS), COLUMNS)


def by_columns(n, step):
    def run(i, carry):
        step(pl.ds(pl.multiple_of(i * COLUMNS, COLUMNS), COLUMNS))
        return carry

    lax.fori_loop(0, n // COLUMNS, run, 0)


def one_way_body(source, mine, inv, base, *refs):
    before, (out, rows, vec, low, cols, far, high, rest) = refs[:-8], refs[-8:]
    n = mine.shape[1]
    at = rows.shape[0] - 1

    def prepare(c):
        if before:
            rows[0, c, :] = before[0][0, c, :]
            vec[0, :, c], low[0, :, c] = before[1][0, :, c], before[2][0, :, c]
        rows[at, c, :] = row_side(source[0:32, c], inv[...]).T
        vec[at, :, c], low[at, :, c] = vector_side(source[32:49, c])
        cols[:, c] = column_side(mine[0:32, c], inv[...])

    far[...] = jnp.full(far.shape, FAR, F32)
    high[...] = jnp.zeros_like(high)
    rest[...] = jnp.zeros_like(rest)
    chunks = n // COLUMNS

    def step(i, carry):
        done = column_step(jnp.maximum(i - 2, 0))
        out[:, done] = base[:, done] + folded(dot(vec[at], high[...]), dot(low[at], rest[...]))[0:17]
        high[...], rest[...] = kernel_values(far[...])
        far[...] = dot(rows[at], cols[:, column_step(jnp.minimum(i, chunks - 1))])
        return carry

    by_columns(n, prepare)
    lax.fori_loop(0, chunks + 2, step, 0)


def estimate(n, passes):
    return pl.CostEstimate(flops=2 * n * n * 256 * passes, bytes_accessed=4 * 115 * n, transcendentals=2 * n * n)


def one_way(source, mine, inv, base, before=()):
    n = mine.shape[1]
    halves = 2 if before else 1
    return pl.pallas_call(
        one_way_body,
        out_shape=(
            jax.ShapeDtypeStruct((17, n), F32),
            jax.ShapeDtypeStruct((halves, n, DEPTH), BF16),
            jax.ShapeDtypeStruct((halves, 48, n), BF16),
            jax.ShapeDtypeStruct((halves, 64, n), LOW),
        ),
        scratch_shapes=[
            pltpu.VMEM((DEPTH, n), BF16),
            pltpu.VMEM((n, COLUMNS), F32),
            pltpu.VMEM((n, COLUMNS), BF16),
            pltpu.VMEM((n, COLUMNS), LOW),
        ],
        cost_estimate=estimate(n, 10),
        compiler_params=pltpu.CompilerParams(vmem_limit_bytes=48 << 20),
    )(source, mine, inv, base, *before)


AXES = ("blk", "half")
MESH = pl.DeviceIdType.MESH


def rounds_body(
    sent, beside, inv, base, rows, vec_r, low_r, own, for_sibling, for_beside, returned, *scratch, route
):
    land, cols, vec_c, low_c, acc, acc_low, par, back, far, high, rest, sems, back_sems = scratch
    n = beside.shape[1]
    parts = n // ROWS
    steps = n // COLUMNS
    mask, last, kind = route
    block, half = lax.axis_index("blk"), lax.axis_index("half")
    core = lax.rem(block, 2)
    bits = {k: lax.rem(lax.div(block, 1 << k), 2) for k in range(last.bit_length()) if (mask | kind) >> k & 1}
    one = block + mask - sum(bits[k] * (2 << k) for k in bits if mask >> k & 1)
    two = last - block
    change = lax.rem(sum(bits[k] for k in bits if kind >> k & 1), 2) * (two - one)
    to, sender = (one + change, half), (two - change, half)

    barrier = pltpu.get_barrier_semaphore()
    for device in (to, sender):
        pl.semaphore_signal(barrier, inc=1, device_id=device, device_id_type=MESH)
    pl.semaphore_wait(barrier, 2)
    fetch = pltpu.make_async_remote_copy(
        src_ref=sent,
        dst_ref=land.at[1],
        send_sem=sems.at[0],
        recv_sem=sems.at[1],
        device_id=to,
        device_id_type=MESH,
    )
    fetch.start()

    def give(i):
        c = pl.ds(pl.multiple_of(i * COLUMNS, COLUMNS), COLUMNS)
        return pltpu.make_async_remote_copy(
            src_ref=par.at[1, :, c],
            dst_ref=back.at[:, c],
            send_sem=back_sems.at[0, i],
            recv_sem=back_sems.at[1, i],
            device_id=sender,
            device_id_type=MESH,
        )

    def clear(c):
        land[0, :, c] = beside[:, c]
        acc[:, :, c] = jnp.zeros((2, 48, COLUMNS), F32)
        acc_low[:, :, c] = jnp.zeros((2, 64, COLUMNS), F32)
        par[:, :, c] = jnp.zeros((2, 24, COLUMNS), F32)

    by_columns(n, clear)

    first = steps * parts
    tiles = 3 * first

    def place(i):
        late = lax.div(lax.div(i, first) + 1, 2)
        left = i - late * first
        visits = (1 + late) * parts
        visit = lax.rem(left, visits)
        row = (1 - late) * core + late * lax.div(visit, parts)
        r = pl.ds(pl.multiple_of(lax.rem(visit, parts) * ROWS, ROWS), ROWS)
        return late, visit, row, r, lax.div(left, visits)

    far[...] = jnp.full(far.shape, FAR, F32)
    high[...] = jnp.zeros_like(high)
    rest[...] = jnp.zeros_like(rest)

    def tile(i, carry):
        late, visit, row, r, at = place(i - lax.div(i, tiles) * (i - tiles + 1))
        late_d, visit_d, row_d, r_d, at_d = place((i - 2) * lax.div(i + tiles, tiles + 2))
        c, c_d = column_step(at), column_step(at_d)

        @pl.when(i == first)
        def _():
            fetch.wait()

        @pl.when(visit == 0)
        def _():
            other = land[late, :, c]
            cols[...] = column_side(other[0:32, :], inv[...])
            vec_c[late, :, c], low_c[late, :, c] = vector_side(other[32:49, :])

        hi, lo = high[...], rest[...]
        par[late_d, :, c_d] += folded(dot(vec_r[row_d, :, r_d], hi), dot(low_r[row_d, :, r_d], lo))
        acc[row_d, :, r_d] += dot_t(vec_c[late_d, :, c_d], hi)
        acc_low[row_d, :, r_d] += dot_t(low_c[late_d, :, c_d], lo)
        high[...], rest[...] = kernel_values(far[...])
        far[...] = dot(rows[row, r, :], cols[...])

        @pl.when(late_d * visit_d == 2 * parts - 1)
        def _():
            give(at_d).start()

        return carry

    lax.fori_loop(0, tiles + 2, tile, 0)

    def total(c):
        own[:, c] = base[:, c] + folded(acc[0, :, c], acc_low[0, :, c])[0:17]
        for_sibling[:, c] = folded(acc[1, :, c], acc_low[1, :, c])[0:17]
        for_beside[:, c] = par[0, 0:17, c]

    def finish(i, carry):
        give(i).wait()
        c = pl.ds(pl.multiple_of(i * COLUMNS, COLUMNS), COLUMNS)
        returned[:, c] = back[0:17, c]
        return carry

    by_columns(n, total)
    lax.fori_loop(0, steps, finish, 0)


def rounds(sent, beside, inv, base, rows, vec, low, route, number):
    n = beside.shape[1]
    steps = n // COLUMNS
    whole = pl.BlockSpec(memory_space=pltpu.VMEM)
    return pl.pallas_call(
        functools.partial(rounds_body, route=route),
        out_shape=(jax.ShapeDtypeStruct((17, n), F32),) * 4,
        in_specs=[whole] * 7,
        out_specs=(whole,) * 4,
        scratch_shapes=[
            pltpu.VMEM((2, 49, n), F32),
            pltpu.VMEM((DEPTH, COLUMNS), BF16),
            pltpu.VMEM((2, 48, n), BF16),
            pltpu.VMEM((2, 64, n), LOW),
            pltpu.VMEM((2, 48, n), F32),
            pltpu.VMEM((2, 64, n), F32),
            pltpu.VMEM((2, 24, n), F32),
            pltpu.VMEM((24, n), F32),
            pltpu.VMEM((ROWS, COLUMNS), F32),
            pltpu.VMEM((ROWS, COLUMNS), BF16),
            pltpu.VMEM((ROWS, COLUMNS), LOW),
            pltpu.SemaphoreType.DMA((2,)),
            pltpu.SemaphoreType.DMA((2, steps)),
        ],
        cost_estimate=estimate(n, 60),
        compiler_params=pltpu.CompilerParams(
            collective_id=number, has_side_effects=True, vmem_limit_bytes=48 << 20
        ),
    )(sent, beside, inv, base, rows, vec, low)


def hops(size, start, flip):
    away = ((start ^ flip) - start) % size
    ways = []
    if away and 2 * away <= size:
        ways.append((0, [(start + k) % size for k in range(away)], 0.5 if 2 * away == size else 1.0))
    if away and 2 * away >= size:
        ways.append((1, [(start - k) % size for k in range(size - away)], 0.5 if 2 * away == size else 1.0))
    return ways


RINGS = ((4, 5, 2), (8, 2, 3), (2, 1, 1))


def loads_of(mask, blocks):
    out = np.zeros((blocks, 3, 2, blocks), np.float32)
    for block in range(blocks):
        at = block
        for axis, (size, low, bits) in enumerate(RINGS):
            field = ((1 << bits) - 1) << low
            for way, places, share in hops(size, (at & field) >> low, (mask & field) >> low):
                for place in places:
                    out[block, axis, way, ((at & ~field) | (place << low)) & ~1] += share
            at = (at & ~field) | ((block ^ mask) & field)
    return out.reshape(blocks, -1)


def parity(x):
    return bin(x).count("1") & 1


def mate_routes(blocks):
    last = blocks - 1
    masks = range(4, blocks, 4)
    loads = {m: loads_of(m, blocks) for m in [*masks, last]}
    kinds = np.array([[parity(w & b) for b in range(blocks)] for w in range(blocks)], np.float32)
    routes = [(2, last, 2)]
    for mask in masks:
        worst = (kinds @ (loads[last] - loads[mask]) + loads[mask].sum(0)).max(1)
        fits = [w for w in range(0, blocks, 4) if parity(w & mask) and parity(w & last)]
        best = min(fits, key=lambda w: (round(float(worst[w]), 3), bin(w).count(str(1)), w))
        routes.append((mask, last, best))
    return routes


def local(points, vectors, inv_length, signal_var, noise_var, masks):
    inv = (inv_length * STRETCH)[:, None]
    mine = jnp.concatenate([points, vectors], axis=0)
    blocks = lax.axis_size("blk")
    last = blocks - 1
    middle = masks[0] ^ masks[1] ^ masks[2] ^ 1 ^ last
    which = middle >> 2
    routes = mate_routes(blocks)
    block = lax.axis_index("blk")
    kind = jnp.int32(0)
    for k in range(last.bit_length()):
        having = sum(1 << i for i, r in enumerate(routes) if r[2] >> k & 1)
        kind = kind ^ (np.uint32(having).astype(np.int32) >> which & block >> k & 1)
    lends = kind == 0
    lent_chip = lends & (middle & 1 == 1)
    lent_far = lends & (middle & 2 == 2) & (which > 0)

    chip = [(b, b ^ 1) for b in range(blocks)]
    apart = [(b, b ^ 2) for b in range(blocks)]
    swap = [(0, 1), (1, 0)]
    beside = lax.ppermute(mine, "blk", chip)
    sibling = lax.ppermute(mine, "half", swap)
    own, *before = one_way(mine, mine, inv, jnp.zeros_like(vectors))
    beside, own = lax.optimization_barrier((beside, own))
    lent = jnp.where(lent_chip, beside, mine)
    across = lax.ppermute(lent, "blk", apart)
    own, *rows = one_way(sibling, mine, inv, own, before)
    across, own = lax.optimization_barrier((across, own))
    sent = jnp.where(lent_far, across, lent)
    ways = [functools.partial(rounds, route=r, number=k) for k, r in enumerate(routes)]
    own, for_sibling, for_beside, returned = lax.switch(which, ways, sent, beside, inv, own, *rows)
    from_sibling = lax.ppermute(for_sibling, "half", swap)
    from_across = lax.ppermute(jnp.where(lent_far, returned, 0.0), "blk", apart)
    kept = jnp.where(lent_far, 0.0, returned) + from_across
    from_beside = lax.ppermute(for_beside + jnp.where(lent_chip, kept, 0.0), "blk", chip)
    sums = own + from_sibling + from_beside + jnp.where(lent_chip, 0.0, kept)
    return (signal_var[0] * FACTOR) * sums + noise_var[0] * vectors


def solution(mesh):
    return jax.shard_map(
        local,
        mesh=mesh,
        in_specs=(P(None, AXES), P(None, AXES), P(), P(), P(), P()),
        out_specs=P(None, AXES),
        check_vma=False,
    )
```

```python
import functools
import math

import jax
import jax.numpy as jnp
import numpy as np
from jax import lax
from jax.experimental import pallas as pl
from jax.experimental.pallas import tpu as pltpu
from jax.sharding import PartitionSpec as P

F32 = jnp.float32
BF16 = jnp.bfloat16
LOW = jnp.float8_e5m2
LOG2E = math.log2(math.e)
ALPHA = 1.5 * LOG2E
BETA = 0.75 * LOG2E * LOG2E
FACTOR = math.exp(1.5) / (3.0 * LOG2E * LOG2E)
STRETCH = math.sqrt(5.0) * LOG2E
TINY = 1e-30
DEPTH = 256
COLUMNS = 256
ROWS = 512
FAR = 1e30
GREETED = 8


def pieces(x, count):
    out = []
    for _ in range(count):
        part = x.astype(BF16).astype(F32)
        out.append(part)
        x = x - part
    return out


def features(points, inv):
    x = points * inv
    norm = jnp.sum(x * x, axis=0, keepdims=True)
    return pieces(x, 3), pieces(norm, 3)


def row_side(points, inv):
    (h, m, l), norm = features(points, inv)
    one = jnp.ones_like(norm[0])
    tail = jnp.concatenate(norm + [one, one, one], axis=0)
    rest = jnp.zeros((DEPTH - 198, points.shape[1]), F32)
    return jnp.concatenate([-2.0 * p for p in (h, h, m, h, l, m)] + [tail, rest], axis=0).astype(BF16)


def column_side(points, inv):
    (h, m, l), norm = features(points, inv)
    one = jnp.ones_like(norm[0])
    tail = jnp.concatenate([one, one, one] + norm, axis=0)
    rest = jnp.zeros((DEPTH - 198, points.shape[1]), F32)
    return jnp.concatenate([h, m, h, l, h, m, tail, rest], axis=0).astype(BF16)


def vector_side(vectors):
    pad = jnp.zeros((7, vectors.shape[1]), F32)
    hi, lo = pieces(vectors, 2)
    wide = jnp.concatenate([hi, pad, lo, pad], axis=0).astype(BF16)
    first = vectors.astype(LOW).astype(F32)
    second = vectors - first
    fill = jnp.zeros((16, vectors.shape[1]), F32)
    low = jnp.concatenate([first, pad, second, pad, fill], axis=0).astype(LOW)
    return wide, low


def kernel_values(squared):
    q = jnp.maximum(squared, TINY)
    h = -ALPHA - q * lax.rsqrt(q)
    values = (h * h + BETA) * jnp.exp2(h)
    hi = values.astype(BF16)
    return hi, (values - hi.astype(F32)).astype(LOW)


def dot(a, b):
    return jnp.dot(a, b, preferred_element_type=F32)


def dot_t(a, b):
    return lax.dot_general(a, b, (((1,), (1,)), ((), ())), preferred_element_type=F32)


def folded(wide, low):
    return wide[0:24] + wide[24:48] + low[0:24] + low[24:48]


def column_step(i):
    return pl.ds(pl.multiple_of(i * COLUMNS, COLUMNS), COLUMNS)


def column_step(i):
    return pl.ds(pl.multiple_of(i * COLUMNS, COLUMNS), COLUMNS)


def by_columns(n, step):
    def run(i, carry):
        step(pl.ds(pl.multiple_of(i * COLUMNS, COLUMNS), COLUMNS))
        return carry

    lax.fori_loop(0, n // COLUMNS, run, 0)


def one_way_body(mine, sibling, inv, out, rows, vec, low, cols):
    n = mine.shape[1]

    def prepare(c):
        for k, side in enumerate((mine, sibling)):
            rows[k, c, :] = row_side(side[0:32, c], inv[...]).T
            vec[k, :, c], low[k, :, c] = vector_side(side[32:49, c])
        cols[:, c] = column_side(mine[0:32, c], inv[...])

    def step(c):
        hi, lo = kernel_values(dot(rows[0], cols[:, c]))
        out[:, c] = folded(dot(vec[0], hi), dot(low[0], lo))[0:17]

    by_columns(n, prepare)
    by_columns(n, step)


def estimate(n, passes):
    return pl.CostEstimate(flops=2 * n * n * 256 * passes, bytes_accessed=4 * 115 * n, transcendentals=2 * n * n)


def one_way(mine, sibling, inv):
    n = mine.shape[1]
    return pl.pallas_call(
        one_way_body,
        out_shape=(
            jax.ShapeDtypeStruct((17, n), F32),
            jax.ShapeDtypeStruct((2, n, DEPTH), BF16),
            jax.ShapeDtypeStruct((2, 48, n), BF16),
            jax.ShapeDtypeStruct((2, 64, n), LOW),
        ),
        scratch_shapes=[pltpu.VMEM((DEPTH, n), BF16)],
        cost_estimate=estimate(n, 10),
        compiler_params=pltpu.CompilerParams(vmem_limit_bytes=48 << 20),
    )(mine, sibling, inv)


AXES = ("blk", "half")
MESH = pl.DeviceIdType.MESH


def rounds_body(
    sent, beside, mine, inv, base, rows, vec_r, low_r, own, for_sibling, for_beside, returned, *scratch, route
):
    land, cols, vec_c, low_c, acc, acc_low, par, back, far, high, rest, sems, back_sems = scratch
    n = beside.shape[1]
    parts = n // ROWS
    steps = n // COLUMNS
    mask, last, kind = route
    block, half = lax.axis_index("blk"), lax.axis_index("half")
    core = lax.rem(block, 2)
    bits = {k: lax.rem(lax.div(block, 1 << k), 2) for k in range(last.bit_length()) if (mask | kind) >> k & 1}
    one = block + mask - sum(bits[k] * (2 << k) for k in bits if mask >> k & 1)
    two = last - block
    change = lax.rem(sum(bits[k] for k in bits if kind >> k & 1), 2) * (two - one)
    to, sender = (one + change, half), (two - change, half)

    barrier = pltpu.get_barrier_semaphore()
    for device in (to, sender):
        pl.semaphore_signal(barrier, inc=1, device_id=device, device_id_type=MESH)
    fetch = pltpu.make_async_remote_copy(
        src_ref=sent,
        dst_ref=land.at[2],
        send_sem=sems.at[0],
        recv_sem=sems.at[1],
        device_id=to,
        device_id_type=MESH,
    )

    def give(i):
        c = pl.ds(pl.multiple_of(i * COLUMNS, COLUMNS), COLUMNS)
        return pltpu.make_async_remote_copy(
            src_ref=par.at[2, :, c],
            dst_ref=back.at[:, c],
            send_sem=back_sems.at[0, i],
            recv_sem=back_sems.at[1, i],
            device_id=sender,
            device_id_type=MESH,
        )

    def clear(c):
        land[0, :, c] = beside[:, c]
        land[1, :, c] = mine[:, c]
        acc[:, :, c] = jnp.zeros((2, 48, COLUMNS), F32)
        acc_low[:, :, c] = jnp.zeros((2, 64, COLUMNS), F32)
        par[:, :, c] = jnp.zeros((3, 24, COLUMNS), F32)

    by_columns(n, clear)

    first = steps * parts
    tiles = 4 * first

    def place(i):
        part = lax.div(i, first)
        late = lax.div(part, 2)
        slot = part - lax.div(part, 3)
        left = i - slot * first
        visits = (1 + late) * parts
        visit = lax.rem(left, visits)
        row = (1 - late) * ((1 - slot) * core + slot) + late * lax.div(visit, parts)
        r = pl.ds(pl.multiple_of(lax.rem(visit, parts) * ROWS, ROWS), ROWS)
        return slot, late * visit, visit, row, r, lax.div(left, visits)

    far[...] = jnp.full(far.shape, FAR, F32)
    high[...] = jnp.zeros_like(high)
    rest[...] = jnp.zeros_like(rest)

    def tile(i, carry):
        slot, _, visit, row, r, at = place(i - lax.div(i, tiles) * (i - tiles + 1))
        slot_d, visit_d, _, row_d, r_d, at_d = place((i - 2) * lax.div(i + tiles, tiles + 2))
        c, c_d = column_step(at), column_step(at_d)

        @pl.when(i == GREETED)
        def _():
            pl.semaphore_wait(barrier, 2)
            fetch.start()

        @pl.when(i == 2 * first)
        def _():
            fetch.wait()

        @pl.when(visit == 0)
        def _():
            other = land[slot, :, c]
            cols[...] = column_side(other[0:32, :], inv[...])
            vec_c[slot, :, c], low_c[slot, :, c] = vector_side(jnp.where(slot == 1, 0.0, other[32:49, :]))

        hi, lo = high[...], rest[...]
        par[slot_d, :, c_d] += folded(dot(vec_r[row_d, :, r_d], hi), dot(low_r[row_d, :, r_d], lo))
        acc[row_d, :, r_d] += dot_t(vec_c[slot_d, :, c_d], hi)
        acc_low[row_d, :, r_d] += dot_t(low_c[slot_d, :, c_d], lo)
        high[...], rest[...] = kernel_values(far[...])
        far[...] = dot(rows[row, r, :], cols[...])

        @pl.when(visit_d == 2 * parts - 1)
        def _():
            give(at_d).start()

        return carry

    lax.fori_loop(0, tiles + 2, tile, 0)

    def total(c):
        own[:, c] = base[:, c] + (par[1, :, c] + folded(acc[0, :, c], acc_low[0, :, c]))[0:17]
        for_sibling[:, c] = folded(acc[1, :, c], acc_low[1, :, c])[0:17]
        for_beside[:, c] = par[0, 0:17, c]

    def finish(i, carry):
        give(i).wait()
        c = pl.ds(pl.multiple_of(i * COLUMNS, COLUMNS), COLUMNS)
        returned[:, c] = back[0:17, c]
        return carry

    by_columns(n, total)
    lax.fori_loop(0, steps, finish, 0)


def rounds(sent, beside, mine, inv, base, rows, vec, low, route, number):
    n = beside.shape[1]
    steps = n // COLUMNS
    whole = pl.BlockSpec(memory_space=pltpu.VMEM)
    return pl.pallas_call(
        functools.partial(rounds_body, route=route),
        out_shape=(jax.ShapeDtypeStruct((17, n), F32),) * 4,
        in_specs=[whole] * 8,
        out_specs=(whole,) * 4,
        scratch_shapes=[
            pltpu.VMEM((3, 49, n), F32),
            pltpu.VMEM((DEPTH, COLUMNS), BF16),
            pltpu.VMEM((3, 48, n), BF16),
            pltpu.VMEM((3, 64, n), LOW),
            pltpu.VMEM((2, 48, n), F32),
            pltpu.VMEM((2, 64, n), F32),
            pltpu.VMEM((3, 24, n), F32),
            pltpu.VMEM((24, n), F32),
            pltpu.VMEM((ROWS, COLUMNS), F32),
            pltpu.VMEM((ROWS, COLUMNS), BF16),
            pltpu.VMEM((ROWS, COLUMNS), LOW),
            pltpu.SemaphoreType.DMA((2,)),
            pltpu.SemaphoreType.DMA((2, steps)),
        ],
        cost_estimate=estimate(n, 80),
        compiler_params=pltpu.CompilerParams(
            collective_id=number, has_side_effects=True, vmem_limit_bytes=48 << 20
        ),
    )(sent, beside, mine, inv, base, rows, vec, low)


def hops(size, start, flip):
    away = ((start ^ flip) - start) % size
    ways = []
    if away and 2 * away <= size:
        ways.append((0, [(start + k) % size for k in range(away)], 0.5 if 2 * away == size else 1.0))
    if away and 2 * away >= size:
        ways.append((1, [(start - k) % size for k in range(size - away)], 0.5 if 2 * away == size else 1.0))
    return ways


RINGS = ((4, 5, 2), (8, 2, 3), (2, 1, 1))


def loads_of(mask, blocks):
    out = np.zeros((blocks, 3, 2, blocks), np.float32)
    for block in range(blocks):
        at = block
        for axis, (size, low, bits) in enumerate(RINGS):
            field = ((1 << bits) - 1) << low
            for way, places, share in hops(size, (at & field) >> low, (mask & field) >> low):
                for place in places:
                    out[block, axis, way, ((at & ~field) | (place << low)) & ~1] += share
            at = (at & ~field) | ((block ^ mask) & field)
    return out.reshape(blocks, -1)


def parity(x):
    return bin(x).count("1") & 1


def mate_routes(blocks):
    last = blocks - 1
    masks = range(4, blocks, 4)
    loads = {m: loads_of(m, blocks) for m in [*masks, last]}
    kinds = np.array([[parity(w & b) for b in range(blocks)] for w in range(blocks)], np.float32)
    routes = [(2, last, 2)]
    for mask in masks:
        worst = (kinds @ (loads[last] - loads[mask]) + loads[mask].sum(0)).max(1)
        fits = [w for w in range(0, blocks, 4) if parity(w & mask) and parity(w & last)]
        best = min(fits, key=lambda w: (round(float(worst[w]), 3), bin(w).count(str(1)), w))
        routes.append((mask, last, best))
    return routes


def local(points, vectors, inv_length, signal_var, noise_var, masks):
    inv = (inv_length * STRETCH)[:, None]
    mine = jnp.concatenate([points, vectors], axis=0)
    blocks = lax.axis_size("blk")
    last = blocks - 1
    middle = masks[0] ^ masks[1] ^ masks[2] ^ 1 ^ last
    which = middle >> 2
    routes = mate_routes(blocks)
    block = lax.axis_index("blk")
    kind = jnp.int32(0)
    for k in range(last.bit_length()):
        having = sum(1 << i for i, r in enumerate(routes) if r[2] >> k & 1)
        kind = kind ^ (np.uint32(having).astype(np.int32) >> which & block >> k & 1)
    lends = kind == 0
    lent_chip = lends & (middle & 1 == 1)
    lent_far = lends & (middle & 2 == 2) & (which > 0)

    chip = [(b, b ^ 1) for b in range(blocks)]
    apart = [(b, b ^ 2) for b in range(blocks)]
    swap = [(0, 1), (1, 0)]
    beside = lax.ppermute(mine, "blk", chip)
    sibling = lax.ppermute(mine, "half", swap)
    lent = jnp.where(lent_chip, beside, mine)
    across = lax.ppermute(lent, "blk", apart)
    first, lent, sibling = lax.optimization_barrier((mine, lent, sibling))
    own, *rows = one_way(first, sibling, inv)
    across, own = lax.optimization_barrier((across, own))
    sent = jnp.where(lent_far, across, lent)
    ways = [functools.partial(rounds, route=r, number=k) for k, r in enumerate(routes)]
    own, for_sibling, for_beside, returned = lax.switch(which, ways, sent, beside, mine, inv, own, *rows)
    from_sibling = lax.ppermute(for_sibling, "half", swap)
    from_across = lax.ppermute(jnp.where(lent_far, returned, 0.0), "blk", apart)
    kept = jnp.where(lent_far, 0.0, returned) + from_across
    from_beside = lax.ppermute(for_beside + jnp.where(lent_chip, kept, 0.0), "blk", chip)
    sums = own + from_sibling + from_beside + jnp.where(lent_chip, 0.0, kept)
    return (signal_var[0] * FACTOR) * sums + noise_var[0] * vectors


def solution(mesh):
    return jax.shard_map(
        local,
        mesh=mesh,
        in_specs=(P(None, AXES), P(None, AXES), P(), P(), P(), P()),
        out_specs=P(None, AXES),
        check_vma=False,
    )
```

```python
import functools
import math

import jax
import jax.numpy as jnp
import numpy as np
from jax import lax
from jax.experimental import pallas as pl
from jax.experimental.pallas import tpu as pltpu
from jax.sharding import PartitionSpec as P

F32 = jnp.float32
BF16 = jnp.bfloat16
LOW = jnp.float8_e5m2
LOG2E = math.log2(math.e)
ALPHA = 1.5 * LOG2E
BETA = 0.75 * LOG2E * LOG2E
FACTOR = math.exp(1.5) / (3.0 * LOG2E * LOG2E)
STRETCH = math.sqrt(5.0) * LOG2E
TINY = 1e-30
DEPTH = 256
COLUMNS = 256
ROWS = 512
FAR = 1e30
GREETED = 8


def pieces(x, count):
    out = []
    for _ in range(count):
        part = x.astype(BF16).astype(F32)
        out.append(part)
        x = x - part
    return out


def features(points, inv):
    x = points * inv
    norm = jnp.sum(x * x, axis=0, keepdims=True)
    return pieces(x, 3), pieces(norm, 3)


def row_side(points, inv):
    (h, m, l), norm = features(points, inv)
    one = jnp.ones_like(norm[0])
    tail = jnp.concatenate(norm + [one, one, one], axis=0)
    rest = jnp.zeros((DEPTH - 198, points.shape[1]), F32)
    return jnp.concatenate([-2.0 * p for p in (h, h, m, h, l, m)] + [tail, rest], axis=0).astype(BF16)


def column_side(points, inv):
    (h, m, l), norm = features(points, inv)
    one = jnp.ones_like(norm[0])
    tail = jnp.concatenate([one, one, one] + norm, axis=0)
    rest = jnp.zeros((DEPTH - 198, points.shape[1]), F32)
    return jnp.concatenate([h, m, h, l, h, m, tail, rest], axis=0).astype(BF16)


def vector_side(vectors):
    pad = jnp.zeros((7, vectors.shape[1]), F32)
    hi, lo = pieces(vectors, 2)
    wide = jnp.concatenate([hi, pad, lo, pad], axis=0).astype(BF16)
    first = vectors.astype(LOW).astype(F32)
    second = vectors - first
    fill = jnp.zeros((16, vectors.shape[1]), F32)
    low = jnp.concatenate([first, pad, second, pad, fill], axis=0).astype(LOW)
    return wide, low


def kernel_values(squared):
    q = jnp.maximum(squared, TINY)
    h = -ALPHA - q * lax.rsqrt(q)
    values = (h * h + BETA) * jnp.exp2(h)
    hi = values.astype(BF16)
    return hi, (values - hi.astype(F32)).astype(LOW)


def dot(a, b):
    return jnp.dot(a, b, preferred_element_type=F32)


def dot_t(a, b):
    return lax.dot_general(a, b, (((1,), (1,)), ((), ())), preferred_element_type=F32)


def folded(wide, low):
    return wide[0:24] + wide[24:48] + low[0:24] + low[24:48]


def column_step(i):
    return pl.ds(pl.multiple_of(i * COLUMNS, COLUMNS), COLUMNS)


def column_step(i):
    return pl.ds(pl.multiple_of(i * COLUMNS, COLUMNS), COLUMNS)


def by_columns(n, step):
    def run(i, carry):
        step(pl.ds(pl.multiple_of(i * COLUMNS, COLUMNS), COLUMNS))
        return carry

    lax.fori_loop(0, n // COLUMNS, run, 0)


def one_way_body(mine, sibling, inv, out, rows, vec, low, cols):
    n = mine.shape[1]

    def prepare(c):
        for k, side in enumerate((mine, sibling)):
            rows[k, c, :] = row_side(side[0:32, c], inv[...]).T
            vec[k, :, c], low[k, :, c] = vector_side(side[32:49, c])
        cols[:, c] = column_side(mine[0:32, c], inv[...])

    def step(c):
        hi, lo = kernel_values(dot(rows[0], cols[:, c]))
        out[:, c] = folded(dot(vec[0], hi), dot(low[0], lo))[0:17]

    by_columns(n, prepare)
    by_columns(n, step)


def estimate(n, passes):
    return pl.CostEstimate(flops=2 * n * n * 256 * passes, bytes_accessed=4 * 115 * n, transcendentals=2 * n * n)


def one_way(mine, sibling, inv):
    n = mine.shape[1]
    return pl.pallas_call(
        one_way_body,
        out_shape=(
            jax.ShapeDtypeStruct((17, n), F32),
            jax.ShapeDtypeStruct((2, n, DEPTH), BF16),
            jax.ShapeDtypeStruct((2, 48, n), BF16),
            jax.ShapeDtypeStruct((2, 64, n), LOW),
        ),
        scratch_shapes=[pltpu.VMEM((DEPTH, n), BF16)],
        cost_estimate=estimate(n, 10),
        compiler_params=pltpu.CompilerParams(vmem_limit_bytes=48 << 20),
    )(mine, sibling, inv)


AXES = ("blk", "half")
MESH = pl.DeviceIdType.MESH


def rounds_body(
    sent, beside, mine, inv, base, rows, vec_r, low_r, own, for_sibling, for_beside, returned, *scratch, route
):
    land, cols, vec_c, low_c, acc, acc_low, par, back, far, high, rest, sems, back_sems = scratch
    n = beside.shape[1]
    parts = n // ROWS
    steps = n // COLUMNS
    mask, last, kind = route
    block, half = lax.axis_index("blk"), lax.axis_index("half")
    core = lax.rem(block, 2)
    bits = {k: lax.rem(lax.div(block, 1 << k), 2) for k in range(last.bit_length()) if (mask | kind) >> k & 1}
    one = block + mask - sum(bits[k] * (2 << k) for k in bits if mask >> k & 1)
    two = last - block
    change = lax.rem(sum(bits[k] for k in bits if kind >> k & 1), 2) * (two - one)
    to, sender = (one + change, half), (two - change, half)

    barrier = pltpu.get_barrier_semaphore()
    for device in (to, sender):
        pl.semaphore_signal(barrier, inc=1, device_id=device, device_id_type=MESH)
    def fetch(i):
        c = column_step(i)
        return pltpu.make_async_remote_copy(
            src_ref=sent.at[:, c],
            dst_ref=land.at[2, :, c],
            send_sem=sems.at[0, i],
            recv_sem=sems.at[1, i],
            device_id=to,
            device_id_type=MESH,
        )

    def give(i):
        c = pl.ds(pl.multiple_of(i * COLUMNS, COLUMNS), COLUMNS)
        return pltpu.make_async_remote_copy(
            src_ref=par.at[2, :, c],
            dst_ref=back.at[:, c],
            send_sem=back_sems.at[0, i],
            recv_sem=back_sems.at[1, i],
            device_id=sender,
            device_id_type=MESH,
        )

    def clear(c):
        land[0, :, c] = beside[:, c]
        land[1, :, c] = mine[:, c]
        acc[:, :, c] = jnp.zeros((2, 48, COLUMNS), F32)
        acc_low[:, :, c] = jnp.zeros((2, 64, COLUMNS), F32)
        par[:, :, c] = jnp.zeros((3, 24, COLUMNS), F32)

    by_columns(n, clear)

    first = steps * parts
    tiles = 4 * first

    def place(i):
        part = lax.div(i, first)
        late = lax.div(part, 2)
        slot = part - lax.div(part, 3)
        left = i - slot * first
        visits = (1 + late) * parts
        visit = lax.rem(left, visits)
        row = (1 - late) * ((1 - slot) * core + slot) + late * lax.div(visit, parts)
        r = pl.ds(pl.multiple_of(lax.rem(visit, parts) * ROWS, ROWS), ROWS)
        return slot, late * visit, visit, row, r, lax.div(left, visits)

    far[...] = jnp.full(far.shape, FAR, F32)
    high[...] = jnp.zeros_like(high)
    rest[...] = jnp.zeros_like(rest)

    def tile(i, carry):
        slot, _, visit, row, r, at = place(i - lax.div(i, tiles) * (i - tiles + 1))
        slot_d, visit_d, _, row_d, r_d, at_d = place((i - 2) * lax.div(i + tiles, tiles + 2))
        c, c_d = column_step(at), column_step(at_d)

        @pl.when(i == GREETED)
        def _():
            pl.semaphore_wait(barrier, 2)

            def begin(k, carry):
                fetch(k).start()
                return carry

            lax.fori_loop(0, steps, begin, 0)

        @pl.when(visit + 2 - slot == 0)
        def _():
            fetch(at).wait()

        @pl.when(visit == 0)
        def _():
            other = land[slot, :, c]
            cols[...] = column_side(other[0:32, :], inv[...])
            vec_c[slot, :, c], low_c[slot, :, c] = vector_side(jnp.where(slot == 1, 0.0, other[32:49, :]))

        hi, lo = high[...], rest[...]
        par[slot_d, :, c_d] += folded(dot(vec_r[row_d, :, r_d], hi), dot(low_r[row_d, :, r_d], lo))
        acc[row_d, :, r_d] += dot_t(vec_c[slot_d, :, c_d], hi)
        acc_low[row_d, :, r_d] += dot_t(low_c[slot_d, :, c_d], lo)
        high[...], rest[...] = kernel_values(far[...])
        far[...] = dot(rows[row, r, :], cols[...])

        @pl.when(visit_d == 2 * parts - 1)
        def _():
            give(at_d).start()

        return carry

    lax.fori_loop(0, tiles + 2, tile, 0)

    def total(c):
        own[:, c] = base[:, c] + (par[1, :, c] + folded(acc[0, :, c], acc_low[0, :, c]))[0:17]
        for_sibling[:, c] = folded(acc[1, :, c], acc_low[1, :, c])[0:17]
        for_beside[:, c] = par[0, 0:17, c]

    def finish(i, carry):
        give(i).wait()
        c = pl.ds(pl.multiple_of(i * COLUMNS, COLUMNS), COLUMNS)
        returned[:, c] = back[0:17, c]
        return carry

    by_columns(n, total)
    lax.fori_loop(0, steps, finish, 0)


def rounds(sent, beside, mine, inv, base, rows, vec, low, route, number):
    n = beside.shape[1]
    steps = n // COLUMNS
    whole = pl.BlockSpec(memory_space=pltpu.VMEM)
    return pl.pallas_call(
        functools.partial(rounds_body, route=route),
        out_shape=(jax.ShapeDtypeStruct((17, n), F32),) * 4,
        in_specs=[whole] * 8,
        out_specs=(whole,) * 4,
        scratch_shapes=[
            pltpu.VMEM((3, 49, n), F32),
            pltpu.VMEM((DEPTH, COLUMNS), BF16),
            pltpu.VMEM((3, 48, n), BF16),
            pltpu.VMEM((3, 64, n), LOW),
            pltpu.VMEM((2, 48, n), F32),
            pltpu.VMEM((2, 64, n), F32),
            pltpu.VMEM((3, 24, n), F32),
            pltpu.VMEM((24, n), F32),
            pltpu.VMEM((ROWS, COLUMNS), F32),
            pltpu.VMEM((ROWS, COLUMNS), BF16),
            pltpu.VMEM((ROWS, COLUMNS), LOW),
            pltpu.SemaphoreType.DMA((2, steps)),
            pltpu.SemaphoreType.DMA((2, steps)),
        ],
        cost_estimate=estimate(n, 80),
        compiler_params=pltpu.CompilerParams(
            collective_id=number, has_side_effects=True, vmem_limit_bytes=48 << 20
        ),
    )(sent, beside, mine, inv, base, rows, vec, low)


def hops(size, start, flip):
    away = ((start ^ flip) - start) % size
    ways = []
    if away and 2 * away <= size:
        ways.append((0, [(start + k) % size for k in range(away)], 0.5 if 2 * away == size else 1.0))
    if away and 2 * away >= size:
        ways.append((1, [(start - k) % size for k in range(size - away)], 0.5 if 2 * away == size else 1.0))
    return ways


RINGS = ((4, 5, 2), (8, 2, 3), (2, 1, 1))


def loads_of(mask, blocks):
    out = np.zeros((blocks, 3, 2, blocks), np.float32)
    for block in range(blocks):
        at = block
        for axis, (size, low, bits) in enumerate(RINGS):
            field = ((1 << bits) - 1) << low
            for way, places, share in hops(size, (at & field) >> low, (mask & field) >> low):
                for place in places:
                    out[block, axis, way, ((at & ~field) | (place << low)) & ~1] += share
            at = (at & ~field) | ((block ^ mask) & field)
    return out.reshape(blocks, -1)


def parity(x):
    return bin(x).count("1") & 1


def mate_routes(blocks):
    last = blocks - 1
    masks = range(4, blocks, 4)
    loads = {m: loads_of(m, blocks) for m in [*masks, last]}
    kinds = np.array([[parity(w & b) for b in range(blocks)] for w in range(blocks)], np.float32)
    routes = [(2, last, 2)]
    for mask in masks:
        worst = (kinds @ (loads[last] - loads[mask]) + loads[mask].sum(0)).max(1)
        fits = [w for w in range(0, blocks, 4) if parity(w & mask) and parity(w & last)]
        best = min(fits, key=lambda w: (round(float(worst[w]), 3), bin(w).count(str(1)), w))
        routes.append((mask, last, best))
    return routes


def local(points, vectors, inv_length, signal_var, noise_var, masks):
    inv = (inv_length * STRETCH)[:, None]
    mine = jnp.concatenate([points, vectors], axis=0)
    blocks = lax.axis_size("blk")
    last = blocks - 1
    middle = masks[0] ^ masks[1] ^ masks[2] ^ 1 ^ last
    which = middle >> 2
    routes = mate_routes(blocks)
    block = lax.axis_index("blk")
    kind = jnp.int32(0)
    for k in range(last.bit_length()):
        having = sum(1 << i for i, r in enumerate(routes) if r[2] >> k & 1)
        kind = kind ^ (np.uint32(having).astype(np.int32) >> which & block >> k & 1)
    lends = kind == 0
    lent_chip = lends & (middle & 1 == 1)
    lent_far = lends & (middle & 2 == 2) & (which > 0)

    chip = [(b, b ^ 1) for b in range(blocks)]
    apart = [(b, b ^ 2) for b in range(blocks)]
    swap = [(0, 1), (1, 0)]
    beside = lax.ppermute(mine, "blk", chip)
    sibling = lax.ppermute(mine, "half", swap)
    lent = jnp.where(lent_chip, beside, mine)
    across = lax.ppermute(lent, "blk", apart)
    first, lent, sibling = lax.optimization_barrier((mine, lent, sibling))
    own, *rows = one_way(first, sibling, inv)
    across, own = lax.optimization_barrier((across, own))
    sent = jnp.where(lent_far, across, lent)
    ways = [functools.partial(rounds, route=r, number=k) for k, r in enumerate(routes)]
    own, for_sibling, for_beside, returned = lax.switch(which, ways, sent, beside, mine, inv, own, *rows)
    from_sibling = lax.ppermute(for_sibling, "half", swap)
    from_across = lax.ppermute(jnp.where(lent_far, returned, 0.0), "blk", apart)
    kept = jnp.where(lent_far, 0.0, returned) + from_across
    from_beside = lax.ppermute(for_beside + jnp.where(lent_chip, kept, 0.0), "blk", chip)
    sums = own + from_sibling + from_beside + jnp.where(lent_chip, 0.0, kept)
    return (signal_var[0] * FACTOR) * sums + noise_var[0] * vectors


def solution(mesh):
    return jax.shard_map(
        local,
        mesh=mesh,
        in_specs=(P(None, AXES), P(None, AXES), P(), P(), P(), P()),
        out_specs=P(None, AXES),
        check_vma=False,
    )
```
